128 devices in a mesh: group: 8 (over x, z_hi), replica: 16 (over z_lo, y, core).
Axes of the slice: x: 4, y: 4, z: 4 (z_hi: 2, z_lo: 2; z = z_hi * 2 + z_lo), core: 2. Of those that a mesh axis runs over, the one named last changes fastest.
Arguments:
- tokens: bfloat16 [32768, 1024], P(('group', 'replica')), may hold values from -24 to 24
- norm_gain: bfloat16 [1024], P('group'), may hold values from 0.25 to 1.75
- in_weight: bfloat16 [1024, 3072], P('group'), may hold values from -0.1875 to 0.1875
- conv_weight: bfloat16 [3, 1024], P(None, 'group'), may hold values from -3.5 to 3.5
- out_weight: bfloat16 [1024, 1024], P('group'), may hold values from -0.1875 to 0.1875
- ffn_gain: bfloat16 [1024], P('group'), may hold values from 0.25 to 1.75
- gate_weight: bfloat16 [1024, 4608], P('group'), may hold values from -0.1875 to 0.1875
- up_weight: bfloat16 [1024, 4608], P('group'), may hold values from -0.1875 to 0.1875
- down_weight: bfloat16 [4608, 1024], P('group'), may hold values from -0.1875 to 0.1875
- cotangent: bfloat16 [32768, 1024], P(('group', 'replica')), may hold values from -24 to 24
Outputs:
- block_out: bfloat16 [32768, 1024], P(('group', 'replica'))
- token_input_gradient: float32 [32768, 1024], P(('group', 'replica'))
- norm_gain_grad: float32 [1024], P('group')
- in_weight_grad: float32 [1024, 3072], P('group')
- conv_weight_grad: float32 [3, 1024], P(None, 'group')
- out_weight_grad: float32 [1024, 1024], P('group')
- ffn_gain_grad: float32 [1024], P('group')
- gate_weight_grad: float32 [1024, 4608], P('group')
- up_weight_grad: float32 [1024, 4608], P('group')
- down_weight_grad: float32 [4608, 1024], P('group')
The draws below stay inside these ranges and needn't reach their ends.
All inputs are finite; a program needn't handle non-finite values.
Results may differ from the reference program's by a relative error of at most 0.018.
Values may be sent and summed in bfloat16 or wider, within the bound.
A program may use at most 256 MiB of HBM per device.

```python
import jax
import jax.numpy as jnp
from jax import lax

D = 1024
FF = 4608
KCONV = 3
LENGTH = 2048
TOKEN_TOTAL = 32768


def with_spikes(values, key, source, target, parts, factor):
    owner, partner = [(jnp.arange(values.shape[position]) // (values.shape[position] // parts)).reshape([-1 if axis == position else 1 for axis in range(values.ndim)]) for position in (source, target)]
    chosen = jax.random.permutation(key, parts)[partner]
    strong = (owner == chosen) | (owner == (partner + parts // 2) % parts)
    return jnp.where(strong, factor * values, values)


def steps_of(rng, extent, shards, least, high):
    gain, own = 1.0, jax.random.fold_in(rng, 6)
    for axis_at, shards_of in shards:
        heights = jnp.exp(jax.random.uniform(jax.random.fold_in(own, axis_at), (shards_of,), jnp.float32, least / len(shards), high / len(shards)))
        gain = gain * jnp.repeat(heights, extent[axis_at] // shards_of).reshape([-1 if axis == axis_at else 1 for axis in range(len(extent))])
    return gain


def normal_values(stream_key, shape, deviation, reach, cuts=(), kind=jnp.bfloat16):
    entries = jax.random.normal(stream_key, shape, jnp.float32) * deviation
    if len(cuts) > 0:
        entries = steps_of(stream_key, shape, cuts, -0.22, 0.18) * entries
    return jnp.clip(entries, min=-reach, max=reach).astype(kind)


def gaussian_with(rng, dims, spread, bound, shards, heavy, held_as=jnp.bfloat16):
    values = spread * jax.random.normal(rng, dims, jnp.float32)
    if shards:
        values = values * steps_of(rng, dims, shards, -0.22, 0.18)
    return jnp.clip(with_spikes(values, jax.random.fold_in(rng, 3), *heavy), -bound, bound).astype(held_as)


def setup_inputs(seed: int = 0) -> dict:
    seeds = jax.random.split(jax.random.key(seed), 11)
    tokens = gaussian_with(seeds[0], (TOKEN_TOTAL, D), 1.0, 24.0, ((0, 128),), (0, 1, 128, 5.5))
    norm_gain = jnp.clip(1.0 + 0.15 * jax.random.normal(seeds[1], (D,), jnp.float32), 0.25, 1.75).astype(jnp.bfloat16)
    in_weight = normal_values(seeds[2], (D, 3 * D), D ** -0.5, 0.1875, ((0, 8),))
    conv_weight = normal_values(seeds[3], (KCONV, D), KCONV ** -0.5, 3.5, ((1, 8),))
    out_weight = normal_values(seeds[4], (D, D), D ** -0.5, 0.1875, ((0, 8),))
    ffn_gain = jnp.clip(1.0 + 0.15 * jax.random.normal(seeds[5], (D,), jnp.float32), 0.25, 1.75).astype(jnp.bfloat16)
    gate_weight = normal_values(seeds[6], (D, FF), D ** -0.5, 0.1875, ((0, 8),))
    up_weight = normal_values(seeds[7], (D, FF), D ** -0.5, 0.1875, ((0, 8),))
    down_weight = normal_values(seeds[8], (FF, D), (FF // 4) ** -0.5, 0.1875, ((0, 8),))
    cotangent = gaussian_with(seeds[9], (TOKEN_TOTAL, D), 1.0, 24.0, ((0, 128),), (0, 1, 128, 5.5))
    return dict(tokens=tokens, norm_gain=norm_gain, in_weight=in_weight, conv_weight=conv_weight, out_weight=out_weight, ffn_gain=ffn_gain, gate_weight=gate_weight, up_weight=up_weight, down_weight=down_weight, cotangent=cotangent)


EPSILON = 1e-06
HIGHEST_PRECISE = lax.Precision.HIGHEST

@jax.custom_vjp
def low(v):
    return lax.optimization_barrier(v.astype(jnp.bfloat16)).astype(jnp.float32)

@jax.custom_vjp
def low_back(v):
    return v

def low_keep(v):
    return (low(v), None)

def low_pass(kept, grad):
    return (grad,)

def back_keep(v):
    return (v, None)

def back_low(kept, grad):
    return (low(grad),)
low.defvjp(low_keep, low_pass)
low_back.defvjp(back_keep, back_low)

def project(value_entries, weight_matrix):
    return jnp.einsum('pou,un->pon', value_entries, weight_matrix, precision=HIGHEST_PRECISE)

def forward(hidden_input, gain_one, w_in, w_conv, w_out, gain_two, w_gate, w_up, w_down):
    model_width = hidden_input.shape[-1]
    seq_length = hidden_input.shape[1]
    scale_one = lax.rsqrt(lax.optimization_barrier(jnp.mean(hidden_input * hidden_input, axis=-1, keepdims=True)) + EPSILON)
    normed_one = low(hidden_input * scale_one * gain_one)
    projected = low_back(project(normed_one, w_in))
    b_part = projected[..., :model_width]
    c_part = projected[..., model_width:2 * model_width]
    x_part = projected[..., 2 * model_width:]
    mixed_in = b_part * x_part
    padded = jnp.pad(mixed_in, ((0, 0), (2, 0), (0, 0)))
    conv_out = w_conv[0] * padded[:, :seq_length] + w_conv[1] * padded[:, 1:seq_length + 1] + w_conv[2] * padded[:, 2:]
    gated = low(c_part * conv_out)
    branch = low_back(project(gated, w_out))
    middle = hidden_input + branch
    scale_two = lax.rsqrt(lax.optimization_barrier(jnp.mean(middle * middle, axis=-1, keepdims=True)) + EPSILON)
    normed_two = low(middle * scale_two * gain_two)
    gate_pre = low_back(project(normed_two, w_gate))
    up_pre = low_back(project(normed_two, w_up))
    hidden_act = low(jax.nn.silu(gate_pre) * up_pre)
    return middle + low_back(project(hidden_act, w_down))

def reference(tokens, norm_gain, in_weight, conv_weight, out_weight, ffn_gain, gate_weight, up_weight, down_weight, cotangent):
    seq_count = TOKEN_TOTAL // LENGTH
    per_step = 2 if seq_count % 2 == 0 else 1
    step_count = seq_count // per_step
    inputs = tokens.astype(jnp.float32).reshape(step_count, per_step, LENGTH, D)
    cotangents = cotangent.astype(jnp.float32).reshape(step_count, per_step, LENGTH, D)
    params = tuple((p.astype(jnp.float32) for p in (norm_gain, in_weight, conv_weight, out_weight, ffn_gain, gate_weight, up_weight, down_weight)))

    def advance(totals, pair):
        hidden_input, cotangent_block = pair
        result, pull = jax.vjp(forward, hidden_input, *params)
        grads = pull(cotangent_block)
        totals = tuple((a + b for a, b in zip(totals, grads[1:])))
        return (totals, (result.astype(jnp.bfloat16), grads[0]))
    zero_grads = tuple((jnp.zeros_like(p) for p in params))
    totals, (results, input_grads) = lax.scan(advance, zero_grads, (inputs, cotangents))
    return (results.reshape(TOKEN_TOTAL, D), input_grads.reshape(TOKEN_TOTAL, D), totals[0], totals[1], totals[2], totals[3], totals[4], totals[5], totals[6], totals[7])
```

```python
import functools

import jax
import jax.numpy as jnp
from jax import lax
from jax.experimental import pallas as pl
from jax.experimental.pallas import tpu as pltpu
from jax.sharding import PartitionSpec as P

MESH = pl.DeviceIdType.MESH
EPSILON = 1e-06
BF = jnp.bfloat16
F32 = jnp.float32
D = 1024
SEG = 72
PAD = 80
FS = 8 * PAD
TEAM = 8
ROWS = 256
T = TEAM * ROWS
VLIM = 60 * 2**20


def coords():
    group, replica = lax.axis_index("group"), lax.axis_index("replica")
    return group // 2, group % 2, replica // 8, (replica // 2) % 4, replica % 2


def device(x, zh, zl, y, c):
    return (x * 2 + zh, zl * 8 + y * 2 + c)


def remote(src, dst, send, recv, target):
    return pltpu.make_async_remote_copy(
        src_ref=src, dst_ref=dst, send_sem=send, recv_sem=recv, device_id=target, device_id_type=MESH
    )


def team_peers():
    x, zh, zl, y, c = coords()
    return [device(x, zh, zl, y, 1 - c)] + [device(x, zh, zl, (y + d) % 4, c) for d in (1, 2, 3)]


def group_peers():
    x, zh, zl, y, c = coords()
    return [
        device((x + dx) % 4, (zh + dz) % 2, zl, y, c)
        for dx in range(4)
        for dz in range(2)
        if (dx, dz) != (0, 0)
    ]


def z_peer():
    x, zh, zl, y, c = coords()
    return device(x, zh, 1 - zl, y, c)


def meet(peers):
    barrier = pltpu.get_barrier_semaphore()
    for peer in peers:
        pl.semaphore_signal(barrier, inc=1, device_id=peer, device_id_type=MESH)
    pl.semaphore_wait(barrier, len(peers))


class TeamGather:
    def __init__(self, src, slot, send, recv, local):
        x, zh, zl, y, c = coords()
        self.c, self.y = c, y
        sibling = device(x, zh, zl, y, 1 - c)
        me = 2 * y + c
        self.own = pltpu.make_async_copy(src, slot(me), local)
        self.pair = remote(src, slot(me), send.at[0], recv.at[0], sibling)
        self.out = [
            remote(src, slot(me), send.at[d], recv.at[d], device(x, zh, zl, (y + d) % 4, c))
            for d in (2, 1, 3)
        ]
        self.relay = []
        for d in (1, 3, 2):
            block = slot(2 * ((y + 4 - d) % 4) + c)
            self.relay.append(
                (
                    remote(src, block, send.at[d], recv.at[d], sibling),
                    remote(block, block, send.at[3 + d], recv.at[3 + d], sibling),
                )
            )

    def start(self):
        for copy in self.out:
            copy.start()
        self.pair.start()
        self.own.start()

    def finish(self):
        for arrived, onward in self.relay:
            arrived.wait_recv()
            onward.start()
        self.own.wait()
        self.pair.wait()
        for copy in self.out:
            copy.wait_send()
        for _, onward in self.relay:
            onward.wait()


class GroupGather:
    def __init__(self, src, slot, send, recv, local):
        x, zh, zl, y, c = coords()
        me = x * 2 + zh
        self.own = pltpu.make_async_copy(src, slot(me), local)
        self.out = [
            remote(src, slot(me), send.at[i], recv.at[i], peer) for i, peer in enumerate(group_peers())
        ]

    def start(self):
        for copy in self.out:
            copy.start()
        self.own.start()

    def finish(self):
        self.own.wait()
        for copy in self.out:
            copy.wait()


class GroupScatter:
    def __init__(self, block, land, send, recv):
        x, zh, zl, y, c = coords()
        self.out = []
        i = 0
        for dx in range(4):
            for dz in range(2):
                if (dx, dz) == (0, 0):
                    continue
                to = ((x + dx) % 4) * 2 + (zh + dz) % 2
                peer = device((x + dx) % 4, (zh + dz) % 2, zl, y, c)
                self.out.append(remote(block(to), land.at[i], send.at[i], recv.at[i], peer))
                i += 1

    def start(self):
        for copy in self.out:
            copy.start()

    def finish(self):
        for copy in self.out:
            copy.wait()


def gather_kernel(n_team, n_group, *refs):
    n = n_team + n_group
    srcs, dsts = refs[:n], refs[n : 2 * n]
    tsend, trecv, gsend, grecv, local = refs[2 * n :]
    peers = (team_peers() if n_team else []) + (group_peers() if n_group else [])
    meet(peers)
    jobs = []
    for i in range(n):
        src, dst = srcs[i], dsts[i]
        if i < n_team:
            if dst.shape[0] == TEAM:
                slot = lambda k, dst=dst: dst.at[k]
            else:
                slot = lambda k, dst=dst: dst.at[:, pl.ds(pl.multiple_of(k * 128, 128), 128)]
            jobs.append(TeamGather(src, slot, tsend.at[i], trecv.at[i], local.at[i]))
        else:
            j = i - n_team
            jobs.append(
                GroupGather(src, lambda k, dst=dst: dst.at[k], gsend.at[j], grecv.at[j], local.at[i])
            )
    for job in jobs:
        job.start()
    for job in jobs:
        job.finish()


def gather(team, group, collective_id, name):
    shapes = [
        jax.ShapeDtypeStruct((T, D) if a.shape == (T, 128) else (TEAM,) + a.shape, a.dtype) for a in team
    ]
    shapes += [jax.ShapeDtypeStruct((8,) + a.shape, a.dtype) for a in group]
    n = len(shapes)
    return pl.pallas_call(
        functools.partial(gather_kernel, len(team), len(group)),
        out_shape=shapes,
        in_specs=[pl.BlockSpec(memory_space=pl.ANY)] * n,
        out_specs=[pl.BlockSpec(memory_space=pl.ANY)] * n,
        scratch_shapes=[
            pltpu.SemaphoreType.DMA((max(len(team), 1), 7)),
            pltpu.SemaphoreType.DMA((max(len(team), 1), 7)),
            pltpu.SemaphoreType.DMA((max(len(group), 1), 7)),
            pltpu.SemaphoreType.DMA((max(len(group), 1), 7)),
            pltpu.SemaphoreType.DMA((n,)),
        ],
        compiler_params=pltpu.CompilerParams(
            collective_id=collective_id, has_side_effects=True, vmem_limit_bytes=VLIM
        ),
        name=name,
    )(*team, *group)


def team_sum_kernel(n, *refs):
    srcs, outs = refs[:n], refs[n : 2 * n]
    pair_land, mine, land, send, recv = refs[2 * n :]
    x, zh, zl, y, c = coords()
    sibling = device(x, zh, zl, y, 1 - c)
    meet(team_peers())
    pairs = [[None] * 4 for _ in range(n)]
    for i in range(n):
        for d in (2, 1, 3, 0):
            k = (y + d) % 4
            pairs[i][d] = remote(
                srcs[i].at[2 * k + 1 - c], pair_land.at[i, d], send.at[i, d], recv.at[i, d], sibling
            )
            pairs[i][d].start()
    outgoing = []
    for i in range(n):
        for d in (2, 1, 3, 0):
            k = (y + d) % 4
            pairs[i][d].wait()
            mine[i, d] = (srcs[i][2 * k + c].astype(F32) + pair_land[i, d].astype(F32)).astype(BF)
            if d:
                copy = remote(
                    mine.at[i, d],
                    land.at[i, d - 1],
                    send.at[i, 3 + d],
                    recv.at[i, 3 + d],
                    device(x, zh, zl, k, c),
                )
                copy.start()
                outgoing.append(copy)
    for i in range(n):
        for copy in outgoing[3 * i : 3 * i + 3]:
            copy.wait()
        outs[i][...] = (
            mine[i, 0].astype(F32) + land[i, 0].astype(F32) + land[i, 1].astype(F32) + land[i, 2].astype(F32)
        )


def team_sum(arrays, collective_id, name):
    n = len(arrays)
    return pl.pallas_call(
        functools.partial(team_sum_kernel, n),
        out_shape=[jax.ShapeDtypeStruct((ROWS, D), F32)] * n,
        in_specs=[pl.BlockSpec(memory_space=pltpu.VMEM)] * n,
        out_specs=[pl.BlockSpec(memory_space=pltpu.VMEM)] * n,
        scratch_shapes=[
            pltpu.VMEM((n, 4, ROWS, D), BF),
            pltpu.VMEM((n, 4, ROWS, D), BF),
            pltpu.VMEM((n, 3, ROWS, D), BF),
            pltpu.SemaphoreType.DMA((n, 7)),
            pltpu.SemaphoreType.DMA((n, 7)),
        ],
        compiler_params=pltpu.CompilerParams(
            collective_id=collective_id, has_side_effects=True, vmem_limit_bytes=VLIM
        ),
        name=name,
    )(*arrays)


def grad_sum_kernel(n, *refs):
    srcs, outs = refs[:n], refs[n : 2 * n]
    rest = refs[2 * n :]
    lands, sums, others = rest[:n], rest[n : 2 * n], rest[2 * n : 3 * n]
    gsend, grecv, zsend, zrecv, tsend, trecv, local = rest[3 * n :]
    x, zh, zl, y, c = coords()
    me = x * 2 + zh
    meet(group_peers() + [z_peer()] + team_peers())
    jobs = [
        GroupScatter(lambda k, s=srcs[i]: s.at[k], lands[i], gsend.at[i], grecv.at[i]) for i in range(n)
    ]
    for job in jobs:
        job.start()
    across = []
    for i in range(n):
        jobs[i].finish()
        total = srcs[i][me].astype(F32)
        for k in range(7):
            total += lands[i][k].astype(F32)
        sums[i][0] = total.astype(sums[i].dtype)
        copy = remote(sums[i].at[0], others[i], zsend.at[i], zrecv.at[i], z_peer())
        copy.start()
        across.append(copy)
    gathers = []
    for i in range(n):
        across[i].wait()
        sums[i][1] = (sums[i][0].astype(F32) + others[i][...].astype(F32)).astype(sums[i].dtype)
        job = TeamGather(
            sums[i].at[1], lambda k, o=outs[i]: o.at[k], tsend.at[i], trecv.at[i], local.at[i]
        )
        job.start()
        gathers.append(job)
    for job in gathers:
        job.finish()


def grad_sum(arrays, collective_id, name):
    n = len(arrays)
    return pl.pallas_call(
        functools.partial(grad_sum_kernel, n),
        out_shape=[jax.ShapeDtypeStruct(a.shape, a.dtype) for a in arrays],
        in_specs=[pl.BlockSpec(memory_space=pltpu.VMEM)] * n,
        out_specs=[pl.BlockSpec(memory_space=pltpu.VMEM)] * n,
        scratch_shapes=[pltpu.VMEM((7,) + a.shape[1:], a.dtype) for a in arrays]
        + [pltpu.VMEM((2,) + a.shape[1:], a.dtype) for a in arrays]
        + [pltpu.VMEM(a.shape[1:], a.dtype) for a in arrays]
        + [
            pltpu.SemaphoreType.DMA((n, 7)),
            pltpu.SemaphoreType.DMA((n, 7)),
            pltpu.SemaphoreType.DMA((n,)),
            pltpu.SemaphoreType.DMA((n,)),
            pltpu.SemaphoreType.DMA((n, 7)),
            pltpu.SemaphoreType.DMA((n, 7)),
            pltpu.SemaphoreType.DMA((n,)),
        ],
        compiler_params=pltpu.CompilerParams(
            collective_id=collective_id, has_side_effects=True, vmem_limit_bytes=VLIM
        ),
        name=name,
    )(*arrays)


def rms_scale(v):
    return lax.rsqrt(jnp.mean(v * v, axis=-1, keepdims=True) + EPSILON)


def norm_reverse(v, scale, gain, grad):
    weighted = grad * gain
    return scale * weighted - v * scale * scale * scale * jnp.mean(weighted * v, axis=-1, keepdims=True)


def dot(a, b):
    return jnp.dot(a, b, preferred_element_type=F32)


def contract_rows(left, right):
    return lax.dot_general(left, right, (((0,), (0,)), ((), ())), preferred_element_type=F32)


def back_project(grad, weight):
    return lax.dot_general(grad, weight, (((1,), (1,)), ((), ())), preferred_element_type=F32)


def on_device(
    tokens, norm_gain, in_weight, conv_weight, out_weight, ffn_gain, gate_weight, up_weight, down_weight, cotangent
):
    member = lax.axis_index("replica") % 8
    lanes = member * 128

    w_in_own = jnp.concatenate(
        [lax.dynamic_slice_in_dim(in_weight, part * D + lanes, 128, axis=1) for part in range(3)], axis=1
    )
    column = lax.broadcasted_iota(jnp.int32, (8 * 576, FS), 0)
    place = lax.broadcasted_iota(jnp.int32, (8 * 576, FS), 1)
    chosen = (place % PAD < SEG) & (column == (place // PAD) * 576 + member * SEG + place % PAD)
    pick = chosen.astype(BF)
    gate_own = dot(gate_weight, pick).astype(BF)
    up_own = dot(up_weight, pick).astype(BF)
    down_own = jnp.pad(lax.dynamic_slice_in_dim(down_weight, member * SEG, SEG, axis=0), ((0, PAD - SEG), (0, 0)))
    small_own = jnp.concatenate([norm_gain[None], ffn_gain[None], conv_weight, jnp.zeros((11, 128), BF)], axis=0)

    tok, w_in, w_out, small = gather([tokens], [w_in_own, out_weight, small_own], 0, "gather_tokens")
    w_in = w_in.reshape(D, 384)
    w_out = w_out.reshape(D, D)
    small = small.transpose(1, 0, 2).reshape(16, D).astype(F32)
    gain_one, gain_two = small[0], small[1]
    taps = lax.dynamic_slice_in_dim(small[2:5], lanes, 128, axis=1)

    h0 = tok.reshape(T, D).astype(F32)
    s1 = rms_scale(h0)
    n1 = (h0 * s1 * gain_one).astype(BF)
    p = dot(n1, w_in)
    b_part, c_part, x_part = p[:, :128], p[:, 128:256], p[:, 256:]
    u = b_part * x_part
    up2 = jnp.concatenate([jnp.zeros((2, 128), F32), u], axis=0)
    v = taps[0] * up2[:T] + taps[1] * up2[1 : T + 1] + taps[2] * up2[2:]
    z_own = (c_part * v).astype(BF)

    z, e, w_gate, w_up, w_down = gather(
        [z_own, cotangent], [gate_own, up_own, down_own], 1, "gather_z"
    )
    w_gate, w_up, w_down = w_gate.reshape(D, FS), w_up.reshape(D, FS), w_down.reshape(FS, D)
    e = e.reshape(T, D)

    h1 = h0 + dot(z, w_out)
    s2 = rms_scale(h1)
    n2 = (h1 * s2 * gain_two).astype(BF)
    g = dot(n2, w_gate)
    q = dot(n2, w_up)
    sig = jax.nn.sigmoid(g)
    act = g * sig
    a = (act * q).astype(BF)
    out_share = dot(a, w_down).astype(BF)
    da = back_project(e, w_down)
    dg = (da * q * sig * (1.0 + g * (1.0 - sig))).astype(BF)
    dq = (da * act).astype(BF)
    dn2_share = back_project(dg, w_gate) + back_project(dq, w_up)
    d_gain_two = jnp.sum(dn2_share * h1 * s2, axis=0)
    out_sum, dn2 = team_sum(
        [out_share.reshape(TEAM, ROWS, D), dn2_share.astype(BF).reshape(TEAM, ROWS, D)], 2, "sum_ffn"
    )
    d_gate = contract_rows(n2, dg).astype(BF)
    d_up = contract_rows(n2, dq).astype(BF)
    d_down = contract_rows(a, e).astype(BF)

    h0_own = tokens.astype(F32)
    h1_own = lax.dynamic_slice_in_dim(h1, member * ROWS, ROWS, axis=0)
    s2_own = rms_scale(h1_own)
    block_out = (h1_own + out_sum).astype(BF)
    dh1 = cotangent.astype(F32) + norm_reverse(h1_own, s2_own, gain_two, dn2)
    (do,) = gather([dh1.astype(BF)], [], 3, "gather_do")
    do = do.reshape(T, D)

    d_out = contract_rows(z, lax.dynamic_slice_in_dim(do, lanes, 128, axis=1)).astype(BF)
    dz = back_project(do, lax.dynamic_slice_in_dim(w_out, lanes, 128, axis=0))
    dc = dz * v
    dv = dz * c_part
    d_conv = jnp.stack([jnp.sum(dv * up2[k : T + k], axis=0) for k in range(3)], axis=0)
    after = jnp.concatenate([dv, jnp.zeros((2, 128), F32)], axis=0)
    du = taps[0] * after[2:] + taps[1] * after[1 : T + 1] + taps[2] * after[:T]
    dp = jnp.concatenate([du * x_part, dc, du * b_part], axis=1).astype(BF)
    d_in = contract_rows(n1, dp).astype(BF)
    dn1_share = back_project(dp, w_in)
    d_gain_one = jnp.sum(dn1_share * h0 * s1, axis=0)
    (dn1,) = team_sum([dn1_share.astype(BF).reshape(TEAM, ROWS, D)], 4, "sum_dn1")
    token_grad = dh1 + norm_reverse(h0_own, rms_scale(h0_own), gain_one, dn1)

    d_conv = lax.dynamic_update_slice(jnp.zeros((3, D), F32), d_conv, (0, lanes))
    d_small = jnp.concatenate([d_gain_one[None], d_gain_two[None], d_conv, jnp.zeros((3, D), F32)], axis=0)
    d_small = d_small.reshape(8, 8, 128).transpose(1, 0, 2)
    s_gate, s_up, s_down, s_in, s_out, s_small = grad_sum(
        [
            d_gate.reshape(8, 128, FS),
            d_up.reshape(8, 128, FS),
            d_down.reshape(8, PAD, D),
            d_in.reshape(8, 128, 384),
            d_out.reshape(8, 128, 128),
            d_small,
        ],
        5,
        "sum_grads",
    )

    def columns(s):
        s = s.reshape(8, 128, 8, PAD)[..., :SEG]
        return s.transpose(1, 2, 0, 3).reshape(128, 8 * 576).astype(F32)

    g_in = s_in.reshape(8, 128, 3, 128).transpose(1, 2, 0, 3).reshape(128, 3 * D).astype(F32)
    g_out = s_out.transpose(1, 0, 2).reshape(128, D).astype(F32)
    g_down = s_down[:, :SEG].reshape(576, D).astype(F32)
    g_small = jnp.sum(s_small, axis=0)
    return (
        block_out,
        token_grad,
        g_small[0],
        g_in,
        g_small[2:5],
        g_out,
        g_small[1],
        columns(s_gate),
        columns(s_up),
        g_down,
    )


def solution(mesh):
    tok = P(("group", "replica"), None)
    rows = P("group", None)
    in_specs = (tok, P("group"), rows, P(None, "group"), rows, P("group"), rows, rows, rows, tok)
    out_specs = (tok, tok, P("group"), rows, P(None, "group"), rows, P("group"), rows, rows, rows)
    return jax.shard_map(on_device, mesh=mesh, in_specs=in_specs, out_specs=out_specs, check_vma=False)
```

```python
import functools

import jax
import jax.numpy as jnp
from jax import lax
from jax.experimental import pallas as pl
from jax.experimental.pallas import tpu as pltpu
from jax.sharding import PartitionSpec as P

MESH = pl.DeviceIdType.MESH
EPSILON = 1e-06
BF = jnp.bfloat16
F32 = jnp.float32
D = 1024
SEG = 72
PAD = 80
FS = 8 * PAD
TEAM = 8
ROWS = 256
T = TEAM * ROWS
VLIM = 60 * 2**20


def coords():
    group, replica = lax.axis_index("group"), lax.axis_index("replica")
    return group // 2, group % 2, replica // 8, (replica // 2) % 4, replica % 2


def device(x, zh, zl, y, c):
    return (x * 2 + zh, zl * 8 + y * 2 + c)


def remote(src, dst, send, recv, target):
    return pltpu.make_async_remote_copy(
        src_ref=src, dst_ref=dst, send_sem=send, recv_sem=recv, device_id=target, device_id_type=MESH
    )


def team_peers():
    x, zh, zl, y, c = coords()
    return [device(x, zh, zl, y, 1 - c)] + [device(x, zh, zl, (y + d) % 4, c) for d in (1, 2, 3)]


def group_peers():
    x, zh, zl, y, c = coords()
    return [
        device((x + dx) % 4, (zh + dz) % 2, zl, y, c)
        for dx in range(4)
        for dz in range(2)
        if (dx, dz) != (0, 0)
    ]


def z_peer():
    x, zh, zl, y, c = coords()
    return device(x, zh, 1 - zl, y, c)


def meet(peers):
    barrier = pltpu.get_barrier_semaphore()
    for peer in peers:
        pl.semaphore_signal(barrier, inc=1, device_id=peer, device_id_type=MESH)
    pl.semaphore_wait(barrier, len(peers))


class TeamGather:
    def __init__(self, src, part, send, recv, local):
        x, zh, zl, y, c = coords()
        sibling = device(x, zh, zl, y, 1 - c)
        right, left = device(x, zh, zl, (y + 1) % 4, c), device(x, zh, zl, (y + 3) % 4, c)
        me = 2 * y + c
        before, after, across = 2 * ((y + 3) % 4) + c, 2 * ((y + 1) % 4) + c, 2 * ((y + 2) % 4) + c
        self.own = pltpu.make_async_copy(src, part(me, None), local)

        def hop(source, block, half, k, target):
            return remote(source, part(block, half), send.at[k], recv.at[k], target)

        self.pair = hop(src, me, None, 0, sibling)
        self.out = [hop(src, me, None, 1, right), hop(src, me, None, 2, left)]
        self.near = [hop(src, before, None, 1, right), hop(src, after, None, 2, left)]
        self.onward = [
            hop(part(before, 0), before, 0, 3, right),
            hop(part(after, 1), after, 1, 4, left),
        ]
        self.far = [
            hop(part(across, 0), across, 0, 3, right),
            hop(part(across, 1), across, 1, 4, left),
        ]
        self.handed = [
            hop(part(before, None), before, None, 5, sibling),
            hop(part(after, None), after, None, 6, sibling),
            hop(part(across, 0), across, 0, 7, sibling),
            hop(part(across, 1), across, 1, 8, sibling),
        ]

    def start(self):
        for copy in self.out:
            copy.start()
        self.pair.start()
        self.own.start()

    def step(self):
        for i in range(2):
            self.near[i].wait_recv()
            self.onward[i].start()
            self.handed[i].start()

    def finish(self):
        for i in range(2):
            self.far[i].wait_recv()
            self.handed[2 + i].start()
        self.own.wait()
        self.pair.wait()
        for copy in self.out + self.onward:
            copy.wait_send()
        for copy in self.handed:
            copy.wait()


def block_part(ref):
    rows = ref.shape[1]
    unit = 8 if ref.dtype == F32 else 16
    cut = (rows // 2 + unit - 1) // unit * unit

    def part(i, half):
        if half is None:
            return ref.at[i]
        return ref.at[i, pl.ds(0, cut)] if half == 0 else ref.at[i, pl.ds(cut, rows - cut)]

    return part


def lane_part(ref):
    rows = ref.shape[0]

    def part(i, half):
        lanes = pl.ds(pl.multiple_of(i * 128, 128), 128)
        if half is None:
            return ref.at[:, lanes]
        return ref.at[pl.ds(half * (rows // 2), rows // 2), lanes]

    return part


class GroupGather:
    def __init__(self, src, slot, send, recv, local):
        x, zh, zl, y, c = coords()
        right, left = device((x + 1) % 4, zh, zl, y, c), device((x + 3) % 4, zh, zl, y, c)
        me, partner = 2 * x + zh, 2 * x + 1 - zh
        before, after, across = 2 * ((x + 3) % 4), 2 * ((x + 1) % 4), 2 * ((x + 2) % 4)
        self.own = pltpu.make_async_copy(src, slot(me), local)

        def hop(source, block, k, target):
            return remote(source, slot(block), send.at[k], recv.at[k], target)

        self.pair = hop(src, me, 0, device(x, 1 - zh, zl, y, c))
        self.out = [hop(src, me, 1, right), hop(src, me, 2, left)]
        self.paired = hop(src, partner, 0, right)
        self.second = [hop(slot(partner), partner, 3, right), hop(slot(partner), partner, 4, left)]
        self.first_in = [hop(src, before, 1 + 2 * zh, right), hop(src, after + 1, 4 - 2 * zh, left)]
        self.onward = [hop(slot(before), before, 5, right), hop(slot(after + 1), after + 1, 6, left)]
        self.last_in = [
            hop(src, before + 1, 3 - 2 * zh, right),
            hop(src, after, 2 + 2 * zh, left),
            hop(src, across, 5, right),
            hop(src, across + 1, 6, left),
        ]

    def start(self):
        self.pair.start()
        for copy in self.out:
            copy.start()
        self.own.start()

    def step(self):
        self.paired.wait_recv()
        for copy in self.second:
            copy.start()

    def relay(self):
        for i in range(2):
            self.first_in[i].wait_recv()
            self.onward[i].start()

    def finish(self):
        self.own.wait()
        for copy in self.last_in:
            copy.wait_recv()
        for copy in [self.pair] + self.out + self.second + self.onward:
            copy.wait_send()


class GroupSum:
    def __init__(self, share, out, half_land, land, z_land, stage, send, recv, tsend, trecv, local):
        x, zh, zl, y, c = coords()
        self.share, self.half_land, self.land, self.z_land, self.stage = share, half_land, land, z_land, stage
        right, left = device((x + 1) % 4, zh, zl, y, c), device((x + 3) % 4, zh, zl, y, c)
        far, self.near, self.back = 2 * ((x + 2) % 4), 2 * ((x + 1) % 4), 2 * ((x + 3) % 4)
        self.here, self.zh = 2 * x, zh
        moves = [
            (share.at[far], half_land.at[0], right),
            (share.at[far + 1], half_land.at[1], left),
            (share.at[pl.ds(self.near, 2)], land.at[0], right),
            (share.at[pl.ds(self.back, 2)], land.at[1], left),
            (stage.at[0], z_land.at[0], device(x, 1 - zh, zl, y, c)),
            (stage.at[1], z_land.at[1], device(x, zh, 1 - zl, y, c)),
        ]
        self.hops = [remote(src, dst, send.at[k], recv.at[k], to) for k, (src, dst, to) in enumerate(moves)]
        self.gather = TeamGather(stage.at[2], block_part(out), tsend, trecv, local)

    def far_out(self):
        self.hops[0].start()
        self.hops[1].start()

    def near_out(self):
        share, kind = self.share, self.share.dtype
        self.hops[0].wait_recv()
        share[self.near] = (share[self.near].astype(F32) + self.half_land[0].astype(F32)).astype(kind)
        self.hops[2].start()
        self.hops[1].wait_recv()
        share[self.back + 1] = (share[self.back + 1].astype(F32) + self.half_land[1].astype(F32)).astype(kind)
        self.hops[3].start()

    def ring_total(self, k):
        return self.share[self.here + k].astype(F32) + self.land[0, k].astype(F32) + self.land[1, k].astype(F32)

    def z_out(self):
        self.hops[2].wait_recv()
        self.hops[3].wait_recv()
        self.stage[0] = self.ring_total(1 - self.zh).astype(self.stage.dtype)
        self.hops[4].start()

    def z_lo_out(self):
        own = self.ring_total(self.zh)
        self.hops[4].wait()
        self.stage[1] = (own + self.z_land[0].astype(F32)).astype(self.stage.dtype)
        self.hops[5].start()

    def team_out(self):
        self.hops[5].wait()
        self.stage[2] = (self.stage[1].astype(F32) + self.z_land[1].astype(F32)).astype(self.stage.dtype)
        self.gather.start()

    def finish(self):
        self.gather.finish()
        for k in range(4):
            self.hops[k].wait_send()

    @staticmethod
    def scratch(r, w, kind):
        return [
            pltpu.VMEM((2, r, w), kind),
            pltpu.VMEM((2, 2, r, w), kind),
            pltpu.VMEM((2, r, w), kind),
            pltpu.VMEM((3, r, w), kind),
            pltpu.SemaphoreType.DMA((6,)),
            pltpu.SemaphoreType.DMA((6,)),
            pltpu.SemaphoreType.DMA((9,)),
            pltpu.SemaphoreType.DMA((9,)),
            pltpu.SemaphoreType.DMA(()),
        ]


def pick(i, values):
    out = values[-1]
    for k in range(len(values) - 2, -1, -1):
        out = jnp.where(i == k, values[k], out)
    return out


def front_kernel(
    tokens, cotangent, small_own, in_own, out_own, gu_own, down_own,
    tok, e, w_in, w_out, w_gu, w_down, gains, p, v, z,
    small, z_own, tsend, trecv, gsend, grecv, local, hsend, hrecv,
):
    x, zh, zl, y, c = coords()
    member = 2 * y + c
    meet(team_peers() + x_peers() + [device(x, 1 - zh, zl, y, c)])
    tok_job = TeamGather(tokens, block_part(tok), tsend.at[0], trecv.at[0], local.at[0])
    e_job = TeamGather(cotangent, block_part(e), tsend.at[1], trecv.at[1], local.at[1])
    z_job = TeamGather(z_own, lane_part(z), tsend.at[2], trecv.at[2], local.at[2])
    out_rows = pl.ds(pl.multiple_of(c * 64, 64), 64)
    slots = [
        lambda k: small.at[k],
        lambda k: w_in.at[pl.ds(pl.multiple_of(k * 128, 128), 128)],
        lambda k: w_out.at[k, out_rows],
        lambda k: w_gu.at[pl.ds(pl.multiple_of(k * 128, 128), 128)],
        lambda k: w_down.at[pl.ds(pl.multiple_of(k * PAD, PAD), PAD)],
    ]
    owned = [small_own, in_own, out_own.at[out_rows], gu_own, down_own]
    jobs = [
        GroupGather(src, slot, gsend.at[i], grecv.at[i], local.at[3 + i])
        for i, (src, slot) in enumerate(zip(owned, slots))
    ]
    tok_job.start()
    for job in jobs:
        job.start()
    tok_job.step()
    e_job.start()
    for job in jobs[:3]:
        job.step()
    jobs[0].relay()
    jobs[1].relay()
    tok_job.finish()
    jobs[0].finish()
    jobs[1].finish()
    for job in jobs[3:]:
        job.step()
    jobs[2].relay()
    for g in range(8):
        gains[:, 128 * g : 128 * g + 128] = small[g].astype(F32)
    taps = gains[:, pl.ds(pl.multiple_of(member * 128, 128), 128)]

    def project(b, last):
        rows = pl.ds(pl.multiple_of(b * ROWS, ROWS), ROWS)
        h0 = tok[b].astype(F32)
        n1 = (h0 * rms_scale(h0) * gains[0:1]).astype(BF)
        block = dot(n1, w_in[...])
        p[rows] = block
        mixed = block[:, :128] * block[:, 256:]
        behind = jnp.concatenate([last, mixed], axis=0)
        conv = taps[2:3] * behind[6 : ROWS + 6] + taps[3:4] * behind[7 : ROWS + 7] + taps[4:5] * behind[8:]
        v[rows] = conv
        z_own[rows] = (block[:, 128:256] * conv).astype(BF)
        return mixed[ROWS - 8 :]

    lax.fori_loop(0, 8, project, jnp.zeros((8, 128), F32))
    z_job.start()
    e_job.step()
    jobs[3].relay()
    jobs[4].relay()
    jobs[2].finish()
    handed = remote(w_out.at[:, out_rows], w_out.at[:, out_rows], hsend, hrecv, device(x, zh, zl, y, 1 - c))
    handed.start()
    e_job.finish()
    z_job.step()
    z_job.finish()
    other_rows = pl.ds(pl.multiple_of(64 - c * 64, 64), 64)
    jobs[3].finish()
    jobs[4].finish()
    handed.wait_send()
    remote(w_out.at[:, out_rows], w_out.at[:, other_rows], hsend, hrecv, device(x, zh, zl, y, 1 - c)).wait_recv()


def front(tokens, cotangent, small_own, in_own, out_own, gu_own, down_own, collective_id, name):
    vmem, anywhere = pl.BlockSpec(memory_space=pltpu.VMEM), pl.BlockSpec(memory_space=pl.ANY)
    shape = jax.ShapeDtypeStruct
    return pl.pallas_call(
        front_kernel,
        out_shape=[
            shape((TEAM, ROWS, D), BF),
            shape((TEAM, ROWS, D), BF),
            shape((D, 384), BF),
            shape((8, 128, D), BF),
            shape((D, 2 * FS), BF),
            shape((FS, D), BF),
            shape((16, D), F32),
            shape((T, 384), F32),
            shape((T, 128), F32),
            shape((T, D), BF),
        ],
        in_specs=[anywhere] * 7,
        out_specs=[vmem, anywhere, vmem, anywhere, anywhere, anywhere, vmem, vmem, vmem, anywhere],
        scratch_shapes=[
            pltpu.VMEM((8, 16, 128), BF),
            pltpu.VMEM((T, 128), BF),
            pltpu.SemaphoreType.DMA((3, 9)),
            pltpu.SemaphoreType.DMA((3, 9)),
            pltpu.SemaphoreType.DMA((5, 7)),
            pltpu.SemaphoreType.DMA((5, 7)),
            pltpu.SemaphoreType.DMA((8,)),
            pltpu.SemaphoreType.DMA(()),
            pltpu.SemaphoreType.DMA(()),
        ],
        compiler_params=pltpu.CompilerParams(
            collective_id=collective_id, has_side_effects=True, vmem_limit_bytes=VLIM
        ),
        name=name,
    )(tokens, cotangent, small_own, in_own, out_own, gu_own, down_own)


class TeamSum:
    def __init__(self, share, pair_land, half_land, land, psend, precv, send, recv):
        x, zh, zl, y, c = coords()
        self.share, self.pair_land, self.half_land, self.land = share, pair_land, half_land, land
        sibling = device(x, zh, zl, y, 1 - c)
        right, left = device(x, zh, zl, (y + 1) % 4, c), device(x, zh, zl, (y + 3) % 4, c)
        chips = [(y + d) % 4 for d in (2, 1, 3, 0)]
        self.mine = [2 * k + c for k in chips]
        self.pairs = [
            remote(share.at[2 * chips[s] + 1 - c], pair_land.at[s], psend.at[s], precv.at[s], sibling)
            for s in range(4)
        ]
        half = ROWS // 2
        far, near, back = self.mine[0], self.mine[1], self.mine[2]
        self.hops = [
            remote(share.at[far, pl.ds(0, half)], half_land.at[0], send.at[0], recv.at[0], right),
            remote(share.at[far, pl.ds(half, half)], half_land.at[1], send.at[1], recv.at[1], left),
            remote(share.at[near], land.at[0], send.at[2], recv.at[2], right),
            remote(share.at[back], land.at[1], send.at[3], recv.at[3], left),
        ]

    def send_pair(self, s):
        self.pairs[s].start()

    def add_pair(self, s):
        share, b = self.share, self.mine[s]
        half = ROWS // 2
        self.pairs[s].wait()
        total = share[b].astype(F32) + self.pair_land[s].astype(F32)
        if s in (1, 2):
            self.hops[s - 1].wait_recv()
            rows = self.half_land[s - 1].astype(F32)
            top, low = total[:half], total[half:]
            if s == 1:
                share[b, :half] = (top + rows).astype(BF)
                share[b, half:] = low.astype(BF)
            else:
                share[b, :half] = top.astype(BF)
                share[b, half:] = (low + rows).astype(BF)
            self.hops[s + 1].start()
        else:
            share[b] = total.astype(BF)
            if s == 0:
                self.hops[0].start()
                self.hops[1].start()

    def result(self):
        for k in (0, 1):
            self.hops[k].wait_send()
        for k in (2, 3):
            self.hops[k].wait()
        b = self.mine[3]
        return self.share[b].astype(F32) + self.land[0].astype(F32) + self.land[1].astype(F32)

    @staticmethod
    def scratch(n):
        return [
            pltpu.VMEM((n, 4, ROWS, D), BF),
            pltpu.VMEM((n, 2, ROWS // 2, D), BF),
            pltpu.VMEM((n, 2, ROWS, D), BF),
            pltpu.SemaphoreType.DMA((n, 4)),
            pltpu.SemaphoreType.DMA((n, 4)),
            pltpu.SemaphoreType.DMA((n, 4)),
            pltpu.SemaphoreType.DMA((n, 4)),
        ]


def ffn_kernel(
    tok_hbm, e_hbm, z_hbm, w_out_hbm, w_gu_hbm, w_down_hbm, gain_ref,
    block_out, dh1_out, do_hbm, d_gu, d_down, gain_grad,
    tok, e, z, w_out, w_gu, w_down, n2, a, dgq, h1_ref, do_own, share, local, wlocal, blocal,
    dsend, drecv, pair_land, half_land, land, psend, precv, send, recv,
):
    x, zh, zl, y, c = coords()
    weights = [
        pltpu.make_async_copy(src, dst, wlocal.at[i])
        for i, (src, dst) in enumerate(((w_out_hbm, w_out), (w_gu_hbm, w_gu), (w_down_hbm, w_down)))
    ]
    blocks = []
    for s, turn in enumerate((2, 1, 3, 0)):
        k = (y + turn) % 4
        pair, rows = pl.ds(2 * k, 2), pl.ds(pl.multiple_of(2 * ROWS * k, 2 * ROWS), 2 * ROWS)
        blocks.append(
            [
                pltpu.make_async_copy(z_hbm.at[rows], z.at[rows], blocal.at[s, 0]),
                pltpu.make_async_copy(tok_hbm.at[pair], tok.at[pair], blocal.at[s, 1]),
                pltpu.make_async_copy(e_hbm.at[pair], e.at[pair], blocal.at[s, 2]),
            ]
        )
    weights[0].start()
    for copy in blocks[0]:
        copy.start()
    for copy in weights[1:]:
        copy.start()
    for copies in blocks[1:]:
        for copy in copies:
            copy.start()
    meet(team_peers())
    sums = [
        TeamSum(
            share.at[k], pair_land.at[k], half_land.at[k], land.at[k],
            psend.at[k], precv.at[k], send.at[k], recv.at[k],
        )
        for k in range(2)
    ]
    for copy in weights:
        copy.wait()
    gain = gain_ref[...]
    gain_grad[...] = jnp.zeros_like(gain_grad)

    def step(i, carry):
        for k in range(4):

            @pl.when(i == 2 * k)
            def _():
                for copy in blocks[k]:
                    copy.wait()

        s, own = i // 2, i % 2
        turn = jnp.where(s == 0, 2, jnp.where(s == 1, 1, jnp.where(s == 2, 3, 0)))
        b = 2 * ((y + turn) % 4) + jnp.where(own == 1, c, 1 - c)
        rows = pl.ds(pl.multiple_of(b * ROWS, ROWS), ROWS)
        h1 = tok[b].astype(F32) + dot(z[rows, :], w_out[...])
        h1_ref[...] = h1
        hs = h1 * lax.rsqrt(jnp.mean(h1 * h1, axis=-1, keepdims=True) + EPSILON)
        n2_b = (hs * gain).astype(BF)
        n2[rows, :] = n2_b
        g = dot(n2_b, w_gu[:, :FS])
        q = dot(n2_b, w_gu[:, FS:])
        sig = jax.nn.sigmoid(g)
        act = g * sig
        a_b = (act * q).astype(BF)
        a[rows, :] = a_b
        da = back_project(e[b], w_down[...])
        dgq[rows, :FS] = (da * q * sig * (1.0 + g * (1.0 - sig))).astype(BF)
        dgq[rows, FS:] = (da * act).astype(BF)
        share[1, b] = dot(a_b, w_down[...]).astype(BF)
        dn2 = back_project(dgq[rows, :], w_gu[...])
        share[0, b] = dn2.astype(BF)
        scale = lax.rsqrt(jnp.mean(h1_ref[...] * h1_ref[...], axis=-1, keepdims=True) + EPSILON)
        gain_grad[...] += jnp.sum(dn2 * (h1_ref[...] * scale), axis=0, keepdims=True)
        for k in range(4):

            @pl.when(i == 2 * k)
            def _():
                sums[0].send_pair(k)
                sums[1].send_pair(k)

            @pl.when(i == 2 * k + 1)
            def _():
                sums[0].add_pair(k)
                sums[1].add_pair(k)

        return carry

    lax.fori_loop(0, 8, step, 0)

    d_down[...] = contract_rows(a[...], e[...].reshape(T, D)).astype(BF)
    dn2 = sums[0].result()
    h1 = h1_ref[...]
    s2 = lax.rsqrt(jnp.mean(h1 * h1, axis=-1, keepdims=True) + EPSILON)
    dh1 = e[2 * y + c].astype(F32) + norm_reverse(h1, s2, gain, dn2)
    dh1_out[...] = dh1
    do_own[...] = dh1.astype(BF)
    do_job = TeamGather(do_own, block_part(do_hbm), dsend, drecv, local)
    do_job.start()

    def tile(m, carry):
        columns = pl.ds(pl.multiple_of(m * 512, 512), 512)
        d_gu[columns, :] = contract_rows(n2[:, columns], dgq[...]).astype(BF)
        return carry

    lax.fori_loop(0, 2, tile, 0)
    do_job.step()
    block_out[...] = (h1_ref[...] + sums[1].result()).astype(BF)
    do_job.finish()


def ffn(tok, e, z, w_out, w_gu, w_down, gain, collective_id, name):
    vmem, anywhere = pl.BlockSpec(memory_space=pltpu.VMEM), pl.BlockSpec(memory_space=pl.ANY)
    shape = jax.ShapeDtypeStruct
    return pl.pallas_call(
        ffn_kernel,
        out_shape=[
            shape((ROWS, D), BF),
            shape((ROWS, D), F32),
            shape((TEAM, ROWS, D), BF),
            shape((D, 2 * FS), BF),
            shape((FS, D), BF),
            shape((1, D), F32),
        ],
        in_specs=[anywhere] * 6 + [vmem],
        out_specs=[vmem, vmem, anywhere, vmem, vmem, vmem],
        scratch_shapes=[
            pltpu.VMEM((TEAM, ROWS, D), BF),
            pltpu.VMEM((TEAM, ROWS, D), BF),
            pltpu.VMEM((T, D), BF),
            pltpu.VMEM((D, D), BF),
            pltpu.VMEM((D, 2 * FS), BF),
            pltpu.VMEM((FS, D), BF),
            pltpu.VMEM((T, D), BF),
            pltpu.VMEM((T, FS), BF),
            pltpu.VMEM((T, 2 * FS), BF),
            pltpu.VMEM((ROWS, D), F32),
            pltpu.VMEM((ROWS, D), BF),
            pltpu.VMEM((2, TEAM, ROWS, D), BF),
            pltpu.SemaphoreType.DMA(()),
            pltpu.SemaphoreType.DMA((3,)),
            pltpu.SemaphoreType.DMA((4, 3)),
            pltpu.SemaphoreType.DMA((9,)),
            pltpu.SemaphoreType.DMA((9,)),
        ]
        + TeamSum.scratch(2),
        compiler_params=pltpu.CompilerParams(
            collective_id=collective_id, has_side_effects=True, vmem_limit_bytes=VLIM
        ),
        name=name,
    )(tok, e, z, w_out, w_gu, w_down, gain)


def conv_back_kernel(
    tok_hbm, do_hbm, z_hbm, d_gu_hbm, d_down_hbm, w_in, w_out_t, p, v, dh1, gains, taps,
    token_grad, gu_out, down_out, in_out, out_out, small_out,
    tok, do, z, d_gu, d_down, d_in, d_out, d_small, n1, up, dv, dp, sums, share, local, *rest,
):
    x, zh, zl, y, c = coords()
    member = 2 * y + c
    here = x * 2 + zh
    meet(team_peers() + x_peers() + [device(x, 1 - zh, zl, y, c), device(x, zh, 1 - zl, y, c)])
    loads = [
        pltpu.make_async_copy(src, dst, local.at[i])
        for i, (src, dst) in enumerate(
            ((d_gu_hbm, d_gu), (d_down_hbm, d_down), (do_hbm, do), (z_hbm, z), (tok_hbm, tok))
        )
    ]
    for copy in loads:
        copy.start()
    dn1_sum = TeamSum(share, *[ref.at[0] for ref in rest[:7]])
    parts = ((d_gu, gu_out), (d_down, down_out), (d_in, in_out), (d_out, out_out), (d_small, small_out))
    jobs = [
        GroupSum(ref, out, *rest[7 + 9 * i : 16 + 9 * i]) for i, (ref, out) in enumerate(parts)
    ]
    gu, down, in_job, out_job, small = jobs
    loads[0].wait()
    gu.far_out()
    loads[1].wait()
    down.far_out()
    loads[2].wait()

    up[pl.ds(0, 8)] = jnp.zeros((8, 128), F32)
    dv[pl.ds(T, 8)] = jnp.zeros((8, 128), F32)

    def first(b, carry):
        rows = pl.ds(pl.multiple_of(b * ROWS, ROWS), ROWS)
        dz = back_project(do[b], w_out_t[...])
        up[pl.ds(pl.multiple_of(b * ROWS, ROWS) + 8, ROWS)] = p[rows, :128] * p[rows, 256:]
        dp[rows, 128:256] = (dz * v[rows]).astype(BF)
        dv[rows] = dz * p[rows, 128:256]
        return carry

    lax.fori_loop(0, 8, first, 0)
    sums[...] = jnp.zeros_like(sums)

    def second(b, carry):
        rows = pl.ds(pl.multiple_of(b * ROWS, ROWS), ROWS)
        longer = pl.ds(pl.multiple_of(b * ROWS, ROWS), ROWS + 8)
        ahead, behind = dv[longer], up[longer]
        du = taps[0:1] * ahead[2 : ROWS + 2] + taps[1:2] * ahead[1 : ROWS + 1] + taps[2:3] * ahead[:ROWS]
        dp[rows, :128] = (du * p[rows, 256:]).astype(BF)
        dp[rows, 256:] = (du * p[rows, :128]).astype(BF)
        for k in range(3):
            sums[2 + k : 3 + k, :128] += jnp.sum(
                ahead[:ROWS] * behind[6 + k : 6 + k + ROWS], axis=0, keepdims=True
            )
        return carry

    lax.fori_loop(0, 8, second, 0)
    gu.near_out()
    down.near_out()
    loads[3].wait()
    d_out[...] = (
        contract_rows(z[...], do[:, :, pl.ds(pl.multiple_of(member * 128, 128), 128)].reshape(T, 128))
        .astype(BF)
        .reshape(8, 128, 128)
    )
    out_job.far_out()
    loads[4].wait()

    def third(i, carry):
        s, own = i // 2, i % 2
        turn = jnp.where(s == 0, 2, jnp.where(s == 1, 1, jnp.where(s == 2, 3, 0)))
        b = 2 * ((y + turn) % 4) + jnp.where(own == 1, c, 1 - c)
        rows = pl.ds(pl.multiple_of(b * ROWS, ROWS), ROWS)
        h0 = tok[b].astype(F32)
        hs = h0 * rms_scale(h0)
        n1[rows, :] = (hs * gains[0:1]).astype(BF)
        dn1 = back_project(dp[rows, :], w_in[...])
        share[b] = dn1.astype(BF)
        sums[0:1] += jnp.sum(dn1 * hs, axis=0, keepdims=True)
        for k in range(4):

            @pl.when(i == 2 * k)
            def _():
                dn1_sum.send_pair(k)

            @pl.when(i == 2 * k + 1)
            def _():
                dn1_sum.add_pair(k)

        return carry

    lax.fori_loop(0, 8, third, 0)
    d_in[...] = contract_rows(n1[...], dp[...]).astype(BF).reshape(8, 128, 384)
    in_job.far_out()
    conv = sums[2:5, :128]
    for g in range(8):
        d_small[g] = jnp.zeros((16, 128), F32)
        d_small[g, 0:1] = sums[0:1, 128 * g : 128 * g + 128]
        d_small[g, 1:2] = gains[1:2, 128 * g : 128 * g + 128]
        d_small[g, 2:5] = jnp.where(member == g, conv, 0.0)
    small.far_out()
    out_job.near_out()
    gu.z_out()
    down.z_out()
    in_job.near_out()
    small.near_out()
    out_job.z_out()
    gu.z_lo_out()
    down.z_lo_out()
    h0 = tok[member].astype(F32)
    token_grad[...] = dh1[...] + norm_reverse(h0, rms_scale(h0), gains[0:1], dn1_sum.result())
    gu.team_out()
    down.team_out()
    out_job.z_lo_out()
    in_job.z_out()
    small.z_out()
    in_job.z_lo_out()
    small.z_lo_out()
    out_job.team_out()
    in_job.team_out()
    small.team_out()
    for job in jobs:
        job.gather.step()
    for job in jobs:
        job.finish()


def x_peers():
    x, zh, zl, y, c = coords()
    return [device((x + 1) % 4, zh, zl, y, c), device((x + 3) % 4, zh, zl, y, c)]


def conv_back(tok, do, z, d_gu, d_down, w_in, w_out_t, p, v, dh1, gains, taps, collective_id, name):
    vmem, anywhere = pl.BlockSpec(memory_space=pltpu.VMEM), pl.BlockSpec(memory_space=pl.ANY)
    shape = jax.ShapeDtypeStruct
    blocks = [((128, 2 * FS), BF), ((PAD, D), BF), ((128, 384), BF), ((128, 128), BF), ((16, 128), F32)]
    scratch = [
        pltpu.VMEM((TEAM, ROWS, D), BF),
        pltpu.VMEM((TEAM, ROWS, D), BF),
        pltpu.VMEM((T, D), BF),
    ]
    scratch += [pltpu.VMEM((8,) + block, kind) for block, kind in blocks]
    scratch += [
        pltpu.VMEM((T, D), BF),
        pltpu.VMEM((T + 8, 128), F32),
        pltpu.VMEM((T + 8, 128), F32),
        pltpu.VMEM((T, 384), BF),
        pltpu.VMEM((8, D), F32),
        pltpu.VMEM((TEAM, ROWS, D), BF),
        pltpu.SemaphoreType.DMA((5,)),
    ]
    scratch += TeamSum.scratch(1)
    for block, kind in blocks:
        scratch += GroupSum.scratch(*block, kind)
    return pl.pallas_call(
        conv_back_kernel,
        out_shape=[shape((ROWS, D), F32)] + [shape((8,) + block, kind) for block, kind in blocks],
        in_specs=[anywhere] * 5 + [vmem] * 7,
        out_specs=[vmem] + [anywhere] * 5,
        scratch_shapes=scratch,
        compiler_params=pltpu.CompilerParams(
            collective_id=collective_id, has_side_effects=True, vmem_limit_bytes=VLIM
        ),
        name=name,
    )(tok, do, z, d_gu, d_down, w_in, w_out_t, p, v, dh1, gains, taps)


def rms_scale(v):
    return lax.rsqrt(jnp.mean(v * v, axis=-1, keepdims=True) + EPSILON)


def norm_reverse(v, scale, gain, grad):
    weighted = grad * gain
    return scale * weighted - v * scale * scale * scale * jnp.mean(weighted * v, axis=-1, keepdims=True)


def dot(a, b):
    return jnp.dot(a, b, preferred_element_type=F32)


def contract_rows(left, right):
    return lax.dot_general(left, right, (((0,), (0,)), ((), ())), preferred_element_type=F32)


def back_project(grad, weight):
    return lax.dot_general(grad, weight, (((1,), (1,)), ((), ())), preferred_element_type=F32)


def on_device(
    tokens, norm_gain, in_weight, conv_weight, out_weight, ffn_gain, gate_weight, up_weight, down_weight, cotangent
):
    member = lax.axis_index("replica") % 8
    lanes = member * 128

    w_in_own = jnp.concatenate(
        [lax.dynamic_slice_in_dim(in_weight, part * D + lanes, 128, axis=1) for part in range(3)], axis=1
    )
    column = lax.broadcasted_iota(jnp.int32, (8 * 576, FS), 0)
    place = lax.broadcasted_iota(jnp.int32, (8 * 576, FS), 1)
    chosen = (place % PAD < SEG) & (column == (place // PAD) * 576 + member * SEG + place % PAD)
    pick = chosen.astype(BF)
    gu_own = jnp.concatenate([dot(gate_weight, pick), dot(up_weight, pick)], axis=1).astype(BF)
    down_own = jnp.pad(lax.dynamic_slice_in_dim(down_weight, member * SEG, SEG, axis=0), ((0, PAD - SEG), (0, 0)))
    small_own = jnp.concatenate([norm_gain[None], ffn_gain[None], conv_weight, jnp.zeros((11, 128), BF)], axis=0)

    tok, e, w_in, w_out, w_gu, w_down, gains, p, v, z = front(
        tokens, cotangent, small_own, w_in_own, out_weight, gu_own, down_own, 0, "front"
    )
    w_out = w_out.reshape(D, D)
    block_out, dh1, do, d_gu, d_down, d_gain_two = ffn(tok, e, z, w_out, w_gu, w_down, gains[1:2], 1, "ffn")
    token_grad, s_gu, s_down, s_in, s_out, s_small = conv_back(
        tok,
        do,
        z,
        d_gu.reshape(8, 128, 2 * FS),
        d_down.reshape(8, PAD, D),
        w_in,
        lax.dynamic_slice_in_dim(w_out, lanes, 128, axis=0),
        p,
        v,
        dh1,
        jnp.concatenate([gains[0:1], d_gain_two, jnp.zeros((6, D), F32)], axis=0),
        jnp.pad(lax.dynamic_slice_in_dim(gains[2:5], lanes, 128, axis=1), ((0, 5), (0, 0))),
        2,
        "conv_back",
    )

    def columns(s):
        s = s.reshape(8, 128, 8, PAD)[..., :SEG]
        return s.transpose(1, 2, 0, 3).reshape(128, 8 * 576).astype(F32)

    g_in = s_in.reshape(8, 128, 3, 128).transpose(1, 2, 0, 3).reshape(128, 3 * D).astype(F32)
    g_out = s_out.transpose(1, 0, 2).reshape(128, D).astype(F32)
    g_down = s_down[:, :SEG].reshape(576, D).astype(F32)
    g_small = jnp.sum(s_small, axis=0)
    return (
        block_out,
        token_grad,
        g_small[0],
        g_in,
        g_small[2:5],
        g_out,
        g_small[1],
        columns(s_gu[..., :FS]),
        columns(s_gu[..., FS:]),
        g_down,
    )


def solution(mesh):
    tok = P(("group", "replica"), None)
    rows = P("group", None)
    in_specs = (tok, P("group"), rows, P(None, "group"), rows, P("group"), rows, rows, rows, tok)
    out_specs = (tok, tok, P("group"), rows, P(None, "group"), rows, P("group"), rows, rows, rows)
    return jax.shard_map(on_device, mesh=mesh, in_specs=in_specs, out_specs=out_specs, check_vma=False)
```

```python
import functools

import jax
import jax.numpy as jnp
from jax import lax
from jax.experimental import pallas as pl
from jax.experimental.pallas import tpu as pltpu
from jax.sharding import PartitionSpec as P

MESH = pl.DeviceIdType.MESH
EPSILON = 1e-06
BF = jnp.bfloat16
F32 = jnp.float32
D = 1024
SEG = 72
PAD = 80
FS = 8 * PAD
TEAM = 8
ROWS = 256
T = TEAM * ROWS
VLIM = 60 * 2**20


def coords():
    group, replica = lax.axis_index("group"), lax.axis_index("replica")
    return group // 2, group % 2, replica // 8, (replica // 2) % 4, replica % 2


def device(x, zh, zl, y, c):
    return (x * 2 + zh, zl * 8 + y * 2 + c)


def remote(src, dst, send, recv, target):
    return pltpu.make_async_remote_copy(
        src_ref=src, dst_ref=dst, send_sem=send, recv_sem=recv, device_id=target, device_id_type=MESH
    )


def team_peers():
    x, zh, zl, y, c = coords()
    return [device(x, zh, zl, y, 1 - c)] + [device(x, zh, zl, (y + d) % 4, c) for d in (1, 2, 3)]


def group_peers():
    x, zh, zl, y, c = coords()
    return [
        device((x + dx) % 4, (zh + dz) % 2, zl, y, c)
        for dx in range(4)
        for dz in range(2)
        if (dx, dz) != (0, 0)
    ]


def z_peer():
    x, zh, zl, y, c = coords()
    return device(x, zh, 1 - zl, y, c)


def meet(peers):
    barrier = pltpu.get_barrier_semaphore()
    for peer in peers:
        pl.semaphore_signal(barrier, inc=1, device_id=peer, device_id_type=MESH)
    pl.semaphore_wait(barrier, len(peers))


class TeamGather:
    def __init__(self, src, part, send, recv, local):
        x, zh, zl, y, c = coords()
        sibling = device(x, zh, zl, y, 1 - c)
        right, left = device(x, zh, zl, (y + 1) % 4, c), device(x, zh, zl, (y + 3) % 4, c)
        me = 2 * y + c
        before, after, across = 2 * ((y + 3) % 4) + c, 2 * ((y + 1) % 4) + c, 2 * ((y + 2) % 4) + c
        self.own = pltpu.make_async_copy(src, part(me, None), local)

        def hop(source, block, half, k, target):
            return remote(source, part(block, half), send.at[k], recv.at[k], target)

        self.pair = hop(src, me, None, 0, sibling)
        self.out = [hop(src, me, None, 1, right), hop(src, me, None, 2, left)]
        self.near = [hop(src, before, None, 1, right), hop(src, after, None, 2, left)]
        self.onward = [
            hop(part(before, 0), before, 0, 3, right),
            hop(part(after, 1), after, 1, 4, left),
        ]
        self.far = [
            hop(part(across, 0), across, 0, 3, right),
            hop(part(across, 1), across, 1, 4, left),
        ]
        self.handed = [
            hop(part(before, None), before, None, 5, sibling),
            hop(part(after, None), after, None, 6, sibling),
            hop(part(across, 0), across, 0, 7, sibling),
            hop(part(across, 1), across, 1, 8, sibling),
        ]

    def start(self):
        for copy in self.out:
            copy.start()
        self.pair.start()
        self.own.start()

    def step(self):
        for i in range(2):
            self.near[i].wait_recv()
            self.onward[i].start()
            self.handed[i].start()

    def near_done(self):
        self.own.wait()
        self.pair.wait()
        for copy in self.handed[:2]:
            copy.wait()

    def hand(self):
        for i in range(2):
            self.far[i].wait_recv()
            self.handed[2 + i].start()

    def far_done(self):
        for copy in self.out + self.onward:
            copy.wait_send()
        for copy in self.handed[2:]:
            copy.wait()

    def finish(self):
        self.hand()
        self.near_done()
        self.far_done()


def block_part(ref):
    rows = ref.shape[1]
    unit = 8 if ref.dtype == F32 else 16
    cut = (rows // 2 + unit - 1) // unit * unit

    def part(i, half):
        if half is None:
            return ref.at[i]
        return ref.at[i, pl.ds(0, cut)] if half == 0 else ref.at[i, pl.ds(cut, rows - cut)]

    return part


def lane_part(ref):
    rows = ref.shape[0]

    def part(i, half):
        lanes = pl.ds(pl.multiple_of(i * 128, 128), 128)
        if half is None:
            return ref.at[:, lanes]
        return ref.at[pl.ds(half * (rows // 2), rows // 2), lanes]

    return part


class GroupGather:
    def __init__(self, src, slot, send, recv, local):
        x, zh, zl, y, c = coords()
        right, left = device((x + 1) % 4, zh, zl, y, c), device((x + 3) % 4, zh, zl, y, c)
        me, partner = 2 * x + zh, 2 * x + 1 - zh
        before, after, across = 2 * ((x + 3) % 4), 2 * ((x + 1) % 4), 2 * ((x + 2) % 4)
        self.own = pltpu.make_async_copy(src, slot(me), local)

        def hop(source, block, k, target):
            return remote(source, slot(block), send.at[k], recv.at[k], target)

        self.pair = hop(src, me, 0, device(x, 1 - zh, zl, y, c))
        self.out = [hop(src, me, 1, right), hop(src, me, 2, left)]
        self.paired = hop(src, partner, 0, right)
        self.second = [hop(slot(partner), partner, 3, right), hop(slot(partner), partner, 4, left)]
        self.first_in = [hop(src, before, 1 + 2 * zh, right), hop(src, after + 1, 4 - 2 * zh, left)]
        self.onward = [hop(slot(before), before, 5, right), hop(slot(after + 1), after + 1, 6, left)]
        self.last_in = [
            hop(src, before + 1, 3 - 2 * zh, right),
            hop(src, after, 2 + 2 * zh, left),
            hop(src, across, 5, right),
            hop(src, across + 1, 6, left),
        ]

    def start(self):
        self.pair.start()
        for copy in self.out:
            copy.start()
        self.own.start()

    def step(self):
        self.paired.wait_recv()
        for copy in self.second:
            copy.start()

    def relay(self):
        for i in range(2):
            self.first_in[i].wait_recv()
            self.onward[i].start()

    def finish(self):
        self.own.wait()
        for copy in self.last_in:
            copy.wait_recv()
        for copy in [self.pair] + self.out + self.second + self.onward:
            copy.wait_send()


class RingSum:
    def __init__(self, share, half_land, land, send, recv):
        x, zh, zl, y, c = coords()
        self.share, self.half_land, self.land = share, half_land, land
        right, left = device((x + 1) % 4, zh, zl, y, c), device((x + 3) % 4, zh, zl, y, c)
        far, self.near, self.back = 2 * ((x + 2) % 4), 2 * ((x + 1) % 4), 2 * ((x + 3) % 4)
        self.here, self.zh = 2 * x, zh
        moves = [
            (share.at[far], half_land.at[0], right),
            (share.at[far + 1], half_land.at[1], left),
            (share.at[pl.ds(self.near, 2)], land.at[0], right),
            (share.at[pl.ds(self.back, 2)], land.at[1], left),
        ]
        self.hops = [remote(src, dst, send.at[k], recv.at[k], to) for k, (src, dst, to) in enumerate(moves)]

    def far_out(self):
        self.hops[0].start()
        self.hops[1].start()

    def near_out(self):
        share, kind = self.share, self.share.dtype
        self.hops[0].wait_recv()
        share[self.near] = (share[self.near].astype(F32) + self.half_land[0].astype(F32)).astype(kind)
        self.hops[2].start()
        self.hops[1].wait_recv()
        share[self.back + 1] = (share[self.back + 1].astype(F32) + self.half_land[1].astype(F32)).astype(kind)
        self.hops[3].start()

    def totals(self, both):
        self.hops[2].wait_recv()
        self.hops[3].wait_recv()
        for i, k in enumerate((1 - self.zh, self.zh)):
            total = self.share[self.here + k].astype(F32)
            total += self.land[0, k].astype(F32) + self.land[1, k].astype(F32)
            both[i] = total.astype(both.dtype)

    def finish(self):
        for hop in self.hops:
            hop.wait_send()

    @staticmethod
    def scratch(r, w, kind):
        return [
            pltpu.VMEM((2, r, w), kind),
            pltpu.VMEM((2, 2, r, w), kind),
            pltpu.SemaphoreType.DMA((4,)),
            pltpu.SemaphoreType.DMA((4,)),
        ]


class PartnerSum:
    def __init__(self, both, out, land, stage, send, recv, tsend, trecv, local):
        x, zh, zl, y, c = coords()
        self.both, self.land, self.stage = both, land, stage
        self.high = remote(both.at[0], land.at[0], send.at[0], recv.at[0], device(x, 1 - zh, zl, y, c))
        self.low = remote(stage.at[0], land.at[1], send.at[1], recv.at[1], device(x, zh, 1 - zl, y, c))
        self.gather = TeamGather(stage.at[1], block_part(out), tsend, trecv, local)

    def z_out(self):
        self.high.start()

    def z_lo_out(self):
        self.high.wait()
        self.stage[0] = (self.both[1].astype(F32) + self.land[0].astype(F32)).astype(self.stage.dtype)
        self.low.start()

    def team_out(self):
        self.low.wait()
        self.stage[1] = (self.stage[0].astype(F32) + self.land[1].astype(F32)).astype(self.stage.dtype)
        self.gather.start()

    @staticmethod
    def scratch(r, w, kind):
        return [
            pltpu.VMEM((2, r, w), kind),
            pltpu.VMEM((2, r, w), kind),
            pltpu.SemaphoreType.DMA((2,)),
            pltpu.SemaphoreType.DMA((2,)),
            pltpu.SemaphoreType.DMA((9,)),
            pltpu.SemaphoreType.DMA((9,)),
            pltpu.SemaphoreType.DMA(()),
        ]


def pick(i, values):
    out = values[-1]
    for k in range(len(values) - 2, -1, -1):
        out = jnp.where(i == k, values[k], out)
    return out


def front_kernel(
    tokens, cotangent, gain_one, in_weight, taps_own, out_own, gain_two, gate_weight, up_weight, down_weight,
    tok, e, w_in, w_out, w_gu, w_down, gains, p, v, z,
    small, small_own, in_own, gu_own, down_own, z_own, tsend, trecv, gsend, grecv, local, hsend, hrecv,
):
    x, zh, zl, y, c = coords()
    member = 2 * y + c
    meet(team_peers() + x_peers() + [device(x, 1 - zh, zl, y, c)])
    tok_job = TeamGather(tokens, block_part(tok), tsend.at[0], trecv.at[0], local.at[0])
    e_job = TeamGather(cotangent, block_part(e), tsend.at[1], trecv.at[1], local.at[1])
    z_job = TeamGather(z_own, lane_part(z), tsend.at[2], trecv.at[2], local.at[2])
    out_rows = pl.ds(pl.multiple_of(c * 64, 64), 64)
    slots = [
        lambda k: small.at[k],
        lambda k: w_in.at[pl.ds(pl.multiple_of(k * 128, 128), 128)],
        lambda k: w_out.at[k, out_rows],
        lambda k: w_gu.at[k],
        lambda k: w_down.at[k],
    ]
    owned = [small_own, in_own, out_own.at[out_rows], gu_own, down_own]
    jobs = [
        GroupGather(src, slot, gsend.at[i], grecv.at[i], local.at[3 + i])
        for i, (src, slot) in enumerate(zip(owned, slots))
    ]
    tok_job.start()
    rows = [gain_one[...].astype(F32), gain_two[...].astype(F32), taps_own[...].astype(F32)]
    small_own[...] = jnp.concatenate(rows + [jnp.zeros((11, 128), F32)], axis=0).astype(BF)
    for part in range(3):
        in_own[:, 128 * part : 128 * part + 128] = in_weight[
            :, pl.ds(pl.multiple_of(part * D + member * 128, 128), 128)
        ]
    for job in jobs[:3]:
        job.start()
    place = lax.broadcasted_iota(jnp.int32, (576, PAD), 1)
    source = lax.broadcasted_iota(jnp.int32, (576, PAD), 0)
    chosen = ((place < SEG) & (source == member * SEG + place)).astype(F32).astype(BF)
    for half, weight in ((0, gate_weight), (FS, up_weight)):
        for g in range(8):
            gu_own[:, half + PAD * g : half + PAD * g + PAD] = dot(
                weight[:, 576 * g : 576 * g + 576], chosen
            ).astype(BF)
    down_own[...] = contract_rows(chosen, down_weight[...]).astype(BF)
    for job in jobs[:3]:
        job.step()
    for job in jobs[:3]:
        job.relay()
    for job in jobs[3:]:
        job.start()
    tok_job.step()
    e_job.start()
    jobs[0].finish()
    jobs[1].finish()
    for g in range(8):
        gains[:, 128 * g : 128 * g + 128] = small[g].astype(F32)
    taps = gains[:, pl.ds(pl.multiple_of(member * 128, 128), 128)]

    def project(i, carry):
        b = 2 * ((y + pick(i // 2, (0, 1, 3, 2))) % 4) + i % 2
        h0 = tok[b].astype(F32)
        n1 = (h0 * rms_scale(h0) * gains[0:1]).astype(BF)
        p[pl.ds(pl.multiple_of(b * ROWS, ROWS), ROWS)] = dot(n1, w_in[...])
        return carry

    tok_job.near_done()
    lax.fori_loop(0, 6, project, 0)
    tok_job.hand()
    tok_job.far_done()
    lax.fori_loop(6, 8, project, 0)
    for job in jobs[3:]:
        job.step()

    def convolve(b, last):
        rows = pl.ds(pl.multiple_of(b * ROWS, ROWS), ROWS)
        block = p[rows]
        mixed = block[:, :128] * block[:, 256:]
        behind = jnp.concatenate([last, mixed], axis=0)
        conv = taps[2:3] * behind[6 : ROWS + 6] + taps[3:4] * behind[7 : ROWS + 7] + taps[4:5] * behind[8:]
        v[rows] = conv
        z_own[rows] = (block[:, 128:256] * conv).astype(BF)
        return mixed[ROWS - 8 :]

    lax.fori_loop(0, 8, convolve, jnp.zeros((8, 128), F32))
    z_job.start()
    e_job.step()
    jobs[3].relay()
    jobs[4].relay()
    jobs[2].finish()
    handed = remote(w_out.at[:, out_rows], w_out.at[:, out_rows], hsend, hrecv, device(x, zh, zl, y, 1 - c))
    handed.start()
    e_job.finish()
    z_job.step()
    z_job.finish()
    other_rows = pl.ds(pl.multiple_of(64 - c * 64, 64), 64)
    jobs[3].finish()
    jobs[4].finish()
    handed.wait_send()
    remote(w_out.at[:, out_rows], w_out.at[:, other_rows], hsend, hrecv, device(x, zh, zl, y, 1 - c)).wait_recv()


def front(args, collective_id, name):
    vmem, anywhere = pl.BlockSpec(memory_space=pltpu.VMEM), pl.BlockSpec(memory_space=pl.ANY)
    shape = jax.ShapeDtypeStruct
    return pl.pallas_call(
        front_kernel,
        out_shape=[
            shape((TEAM, ROWS, D), BF),
            shape((TEAM, ROWS, D), BF),
            shape((D, 384), BF),
            shape((8, 128, D), BF),
            shape((8, 128, 2 * FS), BF),
            shape((8, PAD, D), BF),
            shape((16, D), F32),
            shape((T, 384), F32),
            shape((T, 128), F32),
            shape((T, D), BF),
        ],
        in_specs=[vmem] * 10,
        out_specs=[vmem, anywhere, vmem, anywhere, anywhere, anywhere, vmem, vmem, vmem, anywhere],
        scratch_shapes=[
            pltpu.VMEM((8, 16, 128), BF),
            pltpu.VMEM((16, 128), BF),
            pltpu.VMEM((128, 384), BF),
            pltpu.VMEM((128, 2 * FS), BF),
            pltpu.VMEM((PAD, D), BF),
            pltpu.VMEM((T, 128), BF),
            pltpu.SemaphoreType.DMA((3, 9)),
            pltpu.SemaphoreType.DMA((3, 9)),
            pltpu.SemaphoreType.DMA((5, 7)),
            pltpu.SemaphoreType.DMA((5, 7)),
            pltpu.SemaphoreType.DMA((8,)),
            pltpu.SemaphoreType.DMA(()),
            pltpu.SemaphoreType.DMA(()),
        ],
        compiler_params=pltpu.CompilerParams(
            collective_id=collective_id, has_side_effects=True, vmem_limit_bytes=VLIM
        ),
        name=name,
    )(*args)


class TeamSum:
    def __init__(self, share, pair_land, half_land, land, psend, precv, send, recv):
        x, zh, zl, y, c = coords()
        self.share, self.pair_land, self.half_land, self.land = share, pair_land, half_land, land
        sibling = device(x, zh, zl, y, 1 - c)
        right, left = device(x, zh, zl, (y + 1) % 4, c), device(x, zh, zl, (y + 3) % 4, c)
        chips = [(y + d) % 4 for d in (2, 1, 3, 0)]
        self.mine = [2 * k + c for k in chips]
        self.pairs = [
            remote(share.at[2 * chips[s] + 1 - c], pair_land.at[s], psend.at[s], precv.at[s], sibling)
            for s in range(4)
        ]
        half = ROWS // 2
        far, near, back = self.mine[0], self.mine[1], self.mine[2]
        self.hops = [
            remote(share.at[far, pl.ds(0, half)], half_land.at[0], send.at[0], recv.at[0], right),
            remote(share.at[far, pl.ds(half, half)], half_land.at[1], send.at[1], recv.at[1], left),
            remote(share.at[near], land.at[0], send.at[2], recv.at[2], right),
            remote(share.at[back], land.at[1], send.at[3], recv.at[3], left),
        ]

    def send_pair(self, s):
        self.pairs[s].start()

    def add_pair(self, s):
        share, b = self.share, self.mine[s]
        half = ROWS // 2
        self.pairs[s].wait()
        total = share[b].astype(F32) + self.pair_land[s].astype(F32)
        if s in (1, 2):
            self.hops[s - 1].wait_recv()
            rows = self.half_land[s - 1].astype(F32)
            top, low = total[:half], total[half:]
            if s == 1:
                share[b, :half] = (top + rows).astype(BF)
                share[b, half:] = low.astype(BF)
            else:
                share[b, :half] = top.astype(BF)
                share[b, half:] = (low + rows).astype(BF)
            self.hops[s + 1].start()
        else:
            share[b] = total.astype(BF)
            if s == 0:
                self.hops[0].start()
                self.hops[1].start()

    def result(self):
        for k in (0, 1):
            self.hops[k].wait_send()
        for k in (2, 3):
            self.hops[k].wait()
        b = self.mine[3]
        return self.share[b].astype(F32) + self.land[0].astype(F32) + self.land[1].astype(F32)

    @staticmethod
    def scratch(n):
        return [
            pltpu.VMEM((n, 4, ROWS, D), BF),
            pltpu.VMEM((n, 2, ROWS // 2, D), BF),
            pltpu.VMEM((n, 2, ROWS, D), BF),
            pltpu.SemaphoreType.DMA((n, 4)),
            pltpu.SemaphoreType.DMA((n, 4)),
            pltpu.SemaphoreType.DMA((n, 4)),
            pltpu.SemaphoreType.DMA((n, 4)),
        ]


def ffn_kernel(
    tok_hbm, e_hbm, z_hbm, w_out_hbm, w_gu_hbm, w_down_hbm, gain_ref,
    block_out, dh1_out, do_hbm, gu_both, down_both, gain_grad,
    tok, e, z, w_out, w_gu, w_down, n2, a, dgq, h1_ref, do_own, share, local, wlocal, blocal,
    dsend, drecv, pair_land, half_land, land, psend, precv, send, recv, *rings,
):
    x, zh, zl, y, c = coords()
    weights = [
        pltpu.make_async_copy(src, dst, wlocal.at[i])
        for i, (src, dst) in enumerate(((w_out_hbm, w_out), (w_gu_hbm, w_gu), (w_down_hbm, w_down)))
    ]
    blocks = []
    for s, turn in enumerate((2, 1, 3, 0)):
        k = (y + turn) % 4
        pair, rows = pl.ds(2 * k, 2), pl.ds(pl.multiple_of(2 * ROWS * k, 2 * ROWS), 2 * ROWS)
        blocks.append(
            [
                pltpu.make_async_copy(z_hbm.at[rows], z.at[s % 2], blocal.at[s, 0]),
                pltpu.make_async_copy(tok_hbm.at[pair], tok.at[s % 2], blocal.at[s, 1]),
                pltpu.make_async_copy(e_hbm.at[pair], e.at[pair], blocal.at[s, 2]),
            ]
        )
    weights[0].start()
    for copy in blocks[0]:
        copy.start()
    for copy in weights[1:]:
        copy.start()
    for s, copies in enumerate(blocks[1:]):
        for i, copy in enumerate(copies):
            if i == 2 or s == 0:
                copy.start()
    meet(team_peers() + x_peers())
    gu, down = RingSum(w_gu, *rings[:4]), RingSum(w_down, *rings[4:])
    sums = [
        TeamSum(
            share.at[k], pair_land.at[k], half_land.at[k], land.at[k],
            psend.at[k], precv.at[k], send.at[k], recv.at[k],
        )
        for k in range(2)
    ]
    for copy in weights:
        copy.wait()
    gain = gain_ref[1:2]
    gain_grad[...] = jnp.zeros_like(gain_grad)

    def step(s, carry):
        for k in range(4):

            @pl.when(s == k)
            def _():
                for copy in blocks[k]:
                    copy.wait()
                if k in (1, 2):
                    for copy in blocks[k + 1][:2]:
                        copy.start()

        chip = (y + pick(s, (2, 1, 3, 0))) % 4
        rows = pl.ds(pl.multiple_of(2 * ROWS * chip, 2 * ROWS), 2 * ROWS)
        h1 = tok[s % 2].reshape(2 * ROWS, D).astype(F32) + dot(z[s % 2], w_out[...])
        h1_ref[...] = h1.reshape(2, ROWS, D)
        n2_b = (h1 * rms_scale(h1) * gain).astype(BF)
        n2[rows, :] = n2_b
        g = dot(n2_b, w_gu[:, :, :FS].reshape(D, FS))
        q = dot(n2_b, w_gu[:, :, FS:].reshape(D, FS))
        sig = jax.nn.sigmoid(g)
        act = g * sig
        a[rows, :] = (act * q).astype(BF)
        da = back_project(e[pl.ds(2 * chip, 2)].reshape(2 * ROWS, D), w_down[...].reshape(FS, D))
        dgq[rows, :FS] = (da * q * sig * (1.0 + g * (1.0 - sig))).astype(BF)
        dgq[rows, FS:] = (da * act).astype(BF)
        for k in range(1, 4):

            @pl.when(s == k)
            def _():
                sums[0].add_pair(k - 1)

        for own in range(2):
            core = c if own else 1 - c
            b = 2 * chip + core
            block = pl.ds(pl.multiple_of(b * ROWS, ROWS), ROWS)
            dn2 = back_project(dgq[block, :], w_gu[...].reshape(D, 2 * FS))
            share[0, b] = dn2.astype(BF)
            h1 = h1_ref[core]
            gain_grad[...] += jnp.sum(dn2 * (h1 * rms_scale(h1)), axis=0, keepdims=True)
            share[1, b] = dot(a[block, :], w_down[...].reshape(FS, D)).astype(BF)
            for k in range(4):

                @pl.when(s == k)
                def _():
                    if own:
                        if k:
                            sums[1].add_pair(k - 1)
                    else:
                        sums[0].send_pair(k)
                        sums[1].send_pair(k)

        return carry

    lax.fori_loop(0, 4, step, 0)

    def tile(i, carry):
        m = (((x + 2) % 4) // 2 + i) % 2
        columns = pl.ds(pl.multiple_of(m * 512, 512), 512)
        w_gu[pl.ds(4 * m, 4)] = contract_rows(n2[:, columns], dgq[...]).astype(BF).reshape(4, 128, 2 * FS)

        @pl.when(i == 0)
        def _():
            gu.far_out()

        return carry

    lax.fori_loop(0, 2, tile, 0)
    sums[0].add_pair(3)
    w_down[...] = contract_rows(a[...], e[...].reshape(T, D)).astype(BF).reshape(8, PAD, D)
    gu.near_out()
    down.far_out()
    dn2 = sums[0].result()
    h1 = h1_ref[c]
    dh1 = e[2 * y + c].astype(F32) + norm_reverse(h1, rms_scale(h1), gain, dn2)
    dh1_out[...] = dh1
    do_own[...] = dh1.astype(BF)
    do_job = TeamGather(do_own, block_part(do_hbm), dsend, drecv, local)
    do_job.start()
    sums[1].add_pair(3)
    down.near_out()
    do_job.step()
    block_out[...] = (h1_ref[c] + sums[1].result()).astype(BF)
    do_job.finish()
    gu.totals(gu_both)
    down.totals(down_both)
    gu.finish()
    down.finish()


def ffn(tok, e, z, w_out, w_gu, w_down, gain, collective_id, name):
    vmem, anywhere = pl.BlockSpec(memory_space=pltpu.VMEM), pl.BlockSpec(memory_space=pl.ANY)
    shape = jax.ShapeDtypeStruct
    return pl.pallas_call(
        ffn_kernel,
        out_shape=[
            shape((ROWS, D), BF),
            shape((ROWS, D), F32),
            shape((TEAM, ROWS, D), BF),
            shape((2, 128, 2 * FS), BF),
            shape((2, PAD, D), BF),
            shape((1, D), F32),
        ],
        in_specs=[anywhere] * 6 + [vmem],
        out_specs=[vmem, vmem, anywhere, vmem, vmem, vmem],
        scratch_shapes=[
            pltpu.VMEM((2, 2, ROWS, D), BF),
            pltpu.VMEM((TEAM, ROWS, D), BF),
            pltpu.VMEM((2, 2 * ROWS, D), BF),
            pltpu.VMEM((D, D), BF),
            pltpu.VMEM((8, 128, 2 * FS), BF),
            pltpu.VMEM((8, PAD, D), BF),
            pltpu.VMEM((T, D), BF),
            pltpu.VMEM((T, FS), BF),
            pltpu.VMEM((T, 2 * FS), BF),
            pltpu.VMEM((2, ROWS, D), F32),
            pltpu.VMEM((ROWS, D), BF),
            pltpu.VMEM((2, TEAM, ROWS, D), BF),
            pltpu.SemaphoreType.DMA(()),
            pltpu.SemaphoreType.DMA((3,)),
            pltpu.SemaphoreType.DMA((4, 3)),
            pltpu.SemaphoreType.DMA((9,)),
            pltpu.SemaphoreType.DMA((9,)),
        ]
        + TeamSum.scratch(2)
        + RingSum.scratch(128, 2 * FS, BF)
        + RingSum.scratch(PAD, D, BF),
        compiler_params=pltpu.CompilerParams(
            collective_id=collective_id, has_side_effects=True, vmem_limit_bytes=VLIM
        ),
        name=name,
    )(tok, e, z, w_out, w_gu, w_down, gain)


def conv_back_kernel(
    tok_hbm, do_hbm, z_hbm, w_out_hbm, gu_both, down_both, w_in, p, v, dh1, gains, gain_two_grad,
    token_grad, gu_out, down_out, in_out, out_out, small_out,
    tok, do, z, d_in, d_out, d_small, in_both, out_both, small_both, w_out_t, n1, up, dv, dp, sums, share, local, *rest,
):
    x, zh, zl, y, c = coords()
    member = 2 * y + c
    meet(team_peers() + x_peers() + [device(x, 1 - zh, zl, y, c), device(x, zh, 1 - zl, y, c)])
    loads = [
        pltpu.make_async_copy(src, dst, local.at[i])
        for i, (src, dst) in enumerate(
            (
                (w_out_hbm.at[pl.ds(pl.multiple_of(member * 128, 128), 128)], w_out_t),
                (do_hbm, do),
                (tok_hbm, tok),
                (z_hbm, z),
            )
        )
    ]
    for copy in loads:
        copy.start()
    dn1_sum = TeamSum(share, *[ref.at[0] for ref in rest[:7]])
    in_ring, out_ring, small_ring = [
        RingSum(ref, *rest[7 + 4 * i : 11 + 4 * i]) for i, ref in enumerate((d_in, d_out, d_small))
    ]
    parts = (
        (gu_both, gu_out), (down_both, down_out), (in_both, in_out), (out_both, out_out), (small_both, small_out)
    )
    jobs = [PartnerSum(*part, *rest[19 + 7 * i : 26 + 7 * i]) for i, part in enumerate(parts)]
    gu, down, in_job, out_job, small = jobs
    gu.z_out()
    down.z_out()
    loads[0].wait()
    loads[1].wait()
    taps = gains[:, pl.ds(pl.multiple_of(member * 128, 128), 128)]

    up[pl.ds(0, 8)] = jnp.zeros((8, 128), F32)
    dv[pl.ds(T, 8)] = jnp.zeros((8, 128), F32)

    def first(b, carry):
        rows = pl.ds(pl.multiple_of(b * ROWS, ROWS), ROWS)
        dz = back_project(do[b], w_out_t[...])
        up[pl.ds(pl.multiple_of(b * ROWS, ROWS) + 8, ROWS)] = p[rows, :128] * p[rows, 256:]
        dp[rows, 128:256] = (dz * v[rows]).astype(BF)
        dv[rows] = dz * p[rows, 128:256]
        return carry

    lax.fori_loop(0, 8, first, 0)
    loads[2].wait()
    sums[...] = jnp.zeros_like(sums)

    def second(b, carry):
        rows = pl.ds(pl.multiple_of(b * ROWS, ROWS), ROWS)
        longer = pl.ds(pl.multiple_of(b * ROWS, ROWS), ROWS + 8)
        ahead, behind = dv[longer], up[longer]
        du = taps[2:3] * ahead[2 : ROWS + 2] + taps[3:4] * ahead[1 : ROWS + 1] + taps[4:5] * ahead[:ROWS]
        dp[rows, :128] = (du * p[rows, 256:]).astype(BF)
        dp[rows, 256:] = (du * p[rows, :128]).astype(BF)
        for k in range(3):
            sums[2 + k : 3 + k, :128] += jnp.sum(
                ahead[:ROWS] * behind[6 + k : 6 + k + ROWS], axis=0, keepdims=True
            )
        h0 = tok[b].astype(F32)
        n1[rows, :] = (h0 * rms_scale(h0) * gains[0:1]).astype(BF)
        return carry

    lax.fori_loop(0, 8, second, 0)
    gu.z_lo_out()
    down.z_lo_out()
    def third(i, carry):
        s, own = i // 2, i % 2
        turn = jnp.where(s == 0, 2, jnp.where(s == 1, 1, jnp.where(s == 2, 3, 0)))
        b = 2 * ((y + turn) % 4) + jnp.where(own == 1, c, 1 - c)
        rows = pl.ds(pl.multiple_of(b * ROWS, ROWS), ROWS)
        h0 = tok[b].astype(F32)
        hs = h0 * rms_scale(h0)
        dn1 = back_project(dp[rows, :], w_in[...])
        share[b] = dn1.astype(BF)
        sums[0:1] += jnp.sum(dn1 * hs, axis=0, keepdims=True)
        for k in range(4):

            @pl.when(i == 2 * k)
            def _():
                dn1_sum.send_pair(k)

            @pl.when(i == 2 * k + 1)
            def _():
                dn1_sum.add_pair(k)

        return carry

    lax.fori_loop(0, 8, third, 0)
    gu.team_out()
    d_in[...] = contract_rows(n1[...], dp[...]).astype(BF).reshape(8, 128, 384)
    in_ring.far_out()
    down.team_out()
    loads[3].wait()
    d_out[...] = (
        contract_rows(z[...], do[:, :, pl.ds(pl.multiple_of(member * 128, 128), 128)].reshape(T, 128))
        .astype(BF)
        .reshape(8, 128, 128)
    )
    out_ring.far_out()
    conv = sums[2:5, :128]
    for g in range(8):
        d_small[g] = jnp.zeros((16, 128), F32)
        d_small[g, 0:1] = sums[0:1, 128 * g : 128 * g + 128]
        d_small[g, 1:2] = gain_two_grad[:, 128 * g : 128 * g + 128]
        d_small[g, 2:5] = jnp.where(member == g, conv, 0.0)
    small_ring.far_out()
    in_ring.near_out()
    gu.gather.step()
    out_ring.near_out()
    small_ring.near_out()
    down.gather.step()
    in_ring.totals(in_both)
    in_job.z_out()
    out_ring.totals(out_both)
    out_job.z_out()
    small_ring.totals(small_both)
    small.z_out()
    gu.gather.hand()
    in_job.z_lo_out()
    out_job.z_lo_out()
    down.gather.hand()
    in_job.team_out()
    small.z_lo_out()
    out_job.team_out()
    small.team_out()
    late = (in_job, out_job, small)
    for job in late:
        job.gather.step()
    h0 = tok[member].astype(F32)
    token_grad[...] = dh1[...] + norm_reverse(h0, rms_scale(h0), gains[0:1], dn1_sum.result())
    for job in late:
        job.gather.hand()
    for job in jobs:
        job.gather.near_done()
        job.gather.far_done()
    for ring in (out_ring, in_ring, small_ring):
        ring.finish()


def x_peers():
    x, zh, zl, y, c = coords()
    return [device((x + 1) % 4, zh, zl, y, c), device((x + 3) % 4, zh, zl, y, c)]


def conv_back(args, collective_id, name):
    vmem, anywhere = pl.BlockSpec(memory_space=pltpu.VMEM), pl.BlockSpec(memory_space=pl.ANY)
    shape = jax.ShapeDtypeStruct
    blocks = [((128, 2 * FS), BF), ((PAD, D), BF), ((128, 384), BF), ((128, 128), BF), ((16, 128), F32)]
    scratch = [
        pltpu.VMEM((TEAM, ROWS, D), BF),
        pltpu.VMEM((TEAM, ROWS, D), BF),
        pltpu.VMEM((T, D), BF),
    ]
    scratch += [pltpu.VMEM((8,) + block, kind) for block, kind in blocks[2:]]
    scratch += [pltpu.VMEM((2,) + block, kind) for block, kind in blocks[2:]]
    scratch += [
        pltpu.VMEM((128, D), BF),
        pltpu.VMEM((T, D), BF),
        pltpu.VMEM((T + 8, 128), F32),
        pltpu.VMEM((T + 8, 128), F32),
        pltpu.VMEM((T, 384), BF),
        pltpu.VMEM((8, D), F32),
        pltpu.VMEM((TEAM, ROWS, D), BF),
        pltpu.SemaphoreType.DMA((4,)),
    ]
    scratch += TeamSum.scratch(1)
    for block, kind in blocks[2:]:
        scratch += RingSum.scratch(*block, kind)
    for block, kind in blocks:
        scratch += PartnerSum.scratch(*block, kind)
    return pl.pallas_call(
        conv_back_kernel,
        out_shape=[shape((ROWS, D), F32)] + [shape((8,) + block, kind) for block, kind in blocks],
        in_specs=[anywhere] * 4 + [vmem] * 8,
        out_specs=[vmem] + [anywhere] * 5,
        scratch_shapes=scratch,
        compiler_params=pltpu.CompilerParams(
            collective_id=collective_id, has_side_effects=True, vmem_limit_bytes=VLIM
        ),
        name=name,
    )(*args)


def assemble_kernel(gu, down, w_in, w_out, small, block, token, g_in, g_out, g_gate, g_up, g_down, g_one, g_two, g_conv, b_out, t_out):
    for t in range(TEAM):
        for part in range(3):
            at = part * D + 128 * t
            g_in[:, at : at + 128] = w_in[t, :, 128 * part : 128 * part + 128].astype(F32)
        g_out[:, 128 * t : 128 * t + 128] = w_out[t].astype(F32)
        g_down[SEG * t : SEG * t + SEG, :] = down[t, :SEG].astype(F32)
    total = small[0]
    for t in range(1, TEAM):
        total += small[t]
    g_one[...] = total[0:1]
    g_two[...] = total[1:2]
    g_conv[...] = total[2:5]
    b_out[...] = block[...]
    t_out[...] = token[...]

    def chunk(i, carry):
        rows = pl.ds(pl.multiple_of(i * 32, 32), 32)
        pieces = [gu[t, rows].astype(F32) for t in range(TEAM)]
        for half, ref in ((0, g_gate), (FS, g_up)):
            for g in range(8):
                for t in range(TEAM):
                    at = 576 * g + SEG * t
                    ref[rows, at : at + SEG] = pieces[t][:, half + PAD * g : half + PAD * g + SEG]
        return carry

    lax.fori_loop(0, 4, chunk, 0)


def assemble(gu, down, w_in, w_out, small, block, token):
    vmem, shape = pl.BlockSpec(memory_space=pltpu.VMEM), jax.ShapeDtypeStruct
    return pl.pallas_call(
        assemble_kernel,
        out_shape=[
            shape((128, 3 * D), F32),
            shape((128, D), F32),
            shape((128, 8 * 576), F32),
            shape((128, 8 * 576), F32),
            shape((576, D), F32),
            shape((1, 128), F32),
            shape((1, 128), F32),
            shape((3, 128), F32),
            shape((ROWS, D), BF),
            shape((ROWS, D), F32),
        ],
        in_specs=[vmem] * 7,
        out_specs=[vmem] * 10,
        compiler_params=pltpu.CompilerParams(vmem_limit_bytes=VLIM),
        name="assemble",
    )(gu, down, w_in, w_out, small, block, token)


def rms_scale(v):
    return lax.rsqrt(jnp.mean(v * v, axis=-1, keepdims=True) + EPSILON)


def norm_reverse(v, scale, gain, grad):
    weighted = grad * gain
    return scale * weighted - v * scale * scale * scale * jnp.mean(weighted * v, axis=-1, keepdims=True)


def dot(a, b):
    return jnp.dot(a, b, preferred_element_type=F32)


def contract_rows(left, right):
    return lax.dot_general(left, right, (((0,), (0,)), ((), ())), preferred_element_type=F32)


def back_project(grad, weight):
    return lax.dot_general(grad, weight, (((1,), (1,)), ((), ())), preferred_element_type=F32)


def on_device(
    tokens, norm_gain, in_weight, conv_weight, out_weight, ffn_gain, gate_weight, up_weight, down_weight, cotangent
):
    tok, e, w_in, w_out, w_gu, w_down, gains, p, v, z = front(
        (
            tokens, cotangent, norm_gain[None], in_weight, conv_weight, out_weight, ffn_gain[None],
            gate_weight, up_weight, down_weight,
        ),
        0,
        "front",
    )
    w_out = w_out.reshape(D, D)
    block_out, dh1, do, gu_both, down_both, d_gain_two = ffn(tok, e, z, w_out, w_gu, w_down, gains, 1, "ffn")
    token_grad, s_gu, s_down, s_in, s_out, s_small = conv_back(
        (tok, do, z, w_out, gu_both, down_both, w_in, p, v, dh1, gains, d_gain_two), 2, "conv_back"
    )
    g_in, g_out, g_gate, g_up, g_down, g_one, g_two, g_conv, block_out, token_grad = assemble(
        s_gu, s_down, s_in, s_out, s_small, block_out, token_grad
    )
    return (
        block_out, token_grad, g_one[0], g_in, g_conv, g_out, g_two[0], g_gate, g_up, g_down
    )


def solution(mesh):
    tok = P(("group", "replica"), None)
    rows = P("group", None)
    in_specs = (tok, P("group"), rows, P(None, "group"), rows, P("group"), rows, rows, rows, tok)
    out_specs = (tok, tok, P("group"), rows, P(None, "group"), rows, P("group"), rows, rows, rows)
    return jax.shard_map(on_device, mesh=mesh, in_specs=in_specs, out_specs=out_specs, check_vma=False)
```

```python
import functools

import jax
import jax.numpy as jnp
from jax import lax
from jax.experimental import pallas as pl
from jax.experimental.pallas import tpu as pltpu
from jax.sharding import PartitionSpec as P

MESH = pl.DeviceIdType.MESH
EPSILON = 1e-06
BF = jnp.bfloat16
F32 = jnp.float32
D = 1024
SEG = 72
PAD = 80
FS = 8 * PAD
TEAM = 8
ROWS = 256
T = TEAM * ROWS
VLIM = 60 * 2**20


def coords():
    group, replica = lax.axis_index("group"), lax.axis_index("replica")
    return group // 2, group % 2, replica // 8, (replica // 2) % 4, replica % 2


def device(x, zh, zl, y, c):
    return (x * 2 + zh, zl * 8 + y * 2 + c)


def remote(src, dst, send, recv, target):
    return pltpu.make_async_remote_copy(
        src_ref=src, dst_ref=dst, send_sem=send, recv_sem=recv, device_id=target, device_id_type=MESH
    )


def team_peers():
    x, zh, zl, y, c = coords()
    return [device(x, zh, zl, y, 1 - c)] + [device(x, zh, zl, (y + d) % 4, c) for d in (1, 2, 3)]


def group_peers():
    x, zh, zl, y, c = coords()
    return [
        device((x + dx) % 4, (zh + dz) % 2, zl, y, c)
        for dx in range(4)
        for dz in range(2)
        if (dx, dz) != (0, 0)
    ]


def z_peer():
    x, zh, zl, y, c = coords()
    return device(x, zh, 1 - zl, y, c)


def meet(peers):
    barrier = pltpu.get_barrier_semaphore()
    for peer in peers:
        pl.semaphore_signal(barrier, inc=1, device_id=peer, device_id_type=MESH)
    pl.semaphore_wait(barrier, len(peers))


class TeamGather:
    def __init__(self, src, part, send, recv, local):
        x, zh, zl, y, c = coords()
        sibling = device(x, zh, zl, y, 1 - c)
        right, left = device(x, zh, zl, (y + 1) % 4, c), device(x, zh, zl, (y + 3) % 4, c)
        me = 2 * y + c
        before, after, across = 2 * ((y + 3) % 4) + c, 2 * ((y + 1) % 4) + c, 2 * ((y + 2) % 4) + c
        self.own = pltpu.make_async_copy(src, part(me, None), local)

        def hop(source, block, half, k, target):
            return remote(source, part(block, half), send.at[k], recv.at[k], target)

        self.pair = hop(src, me, None, 0, sibling)
        self.out = [hop(src, me, None, 1, right), hop(src, me, None, 2, left)]
        self.near = [hop(src, before, None, 1, right), hop(src, after, None, 2, left)]
        self.onward = [
            hop(part(before, 0), before, 0, 3, right),
            hop(part(after, 1), after, 1, 4, left),
        ]
        self.far = [
            hop(part(across, 0), across, 0, 3, right),
            hop(part(across, 1), across, 1, 4, left),
        ]
        self.handed = [
            hop(part(before, None), before, None, 5, sibling),
            hop(part(after, None), after, None, 6, sibling),
            hop(part(across, 0), across, 0, 7, sibling),
            hop(part(across, 1), across, 1, 8, sibling),
        ]

    def start(self):
        for copy in self.out:
            copy.start()
        self.pair.start()
        self.own.start()

    def step(self):
        for i in range(2):
            self.near[i].wait_recv()
            self.onward[i].start()
            self.handed[i].start()

    def near_done(self):
        self.own.wait()
        self.pair.wait()
        for copy in self.handed[:2]:
            copy.wait()

    def hand(self):
        for i in range(2):
            self.far[i].wait_recv()
            self.handed[2 + i].start()

    def far_done(self):
        for copy in self.out + self.onward:
            copy.wait_send()
        for copy in self.handed[2:]:
            copy.wait()

    def finish(self):
        self.hand()
        self.near_done()
        self.far_done()


def block_part(ref):
    rows = ref.shape[1]
    unit = 8 if ref.dtype == F32 else 16
    cut = (rows // 2 + unit - 1) // unit * unit

    def part(i, half):
        if half is None:
            return ref.at[i]
        return ref.at[i, pl.ds(0, cut)] if half == 0 else ref.at[i, pl.ds(cut, rows - cut)]

    return part


def lane_part(ref):
    rows = ref.shape[0]

    def part(i, half):
        lanes = pl.ds(pl.multiple_of(i * 128, 128), 128)
        if half is None:
            return ref.at[:, lanes]
        return ref.at[pl.ds(half * (rows // 2), rows // 2), lanes]

    return part


class GroupGather:
    def __init__(self, src, slot, send, recv, local):
        x, zh, zl, y, c = coords()
        right, left = device((x + 1) % 4, zh, zl, y, c), device((x + 3) % 4, zh, zl, y, c)
        me, partner = 2 * x + zh, 2 * x + 1 - zh
        before, after, across = 2 * ((x + 3) % 4), 2 * ((x + 1) % 4), 2 * ((x + 2) % 4)
        self.own = pltpu.make_async_copy(src, slot(me), local)

        def hop(source, block, k, target):
            return remote(source, slot(block), send.at[k], recv.at[k], target)

        self.pair = hop(src, me, 0, device(x, 1 - zh, zl, y, c))
        self.out = [hop(src, me, 1, right), hop(src, me, 2, left)]
        self.paired = hop(src, partner, 0, right)
        self.second = [hop(slot(partner), partner, 3, right), hop(slot(partner), partner, 4, left)]
        self.first_in = [hop(src, before, 1 + 2 * zh, right), hop(src, after + 1, 4 - 2 * zh, left)]
        self.onward = [hop(slot(before), before, 5, right), hop(slot(after + 1), after + 1, 6, left)]
        self.last_in = [
            hop(src, before + 1, 3 - 2 * zh, right),
            hop(src, after, 2 + 2 * zh, left),
            hop(src, across, 5, right),
            hop(src, across + 1, 6, left),
        ]

    def start(self):
        self.pair.start()
        for copy in self.out:
            copy.start()
        self.own.start()

    def step(self):
        self.paired.wait_recv()
        for copy in self.second:
            copy.start()

    def relay(self):
        for i in range(2):
            self.first_in[i].wait_recv()
            self.onward[i].start()

    def finish(self):
        self.own.wait()
        for copy in self.last_in:
            copy.wait_recv()
        for copy in [self.pair] + self.out + self.second + self.onward:
            copy.wait_send()


class RingSum:
    def __init__(self, share, half_land, land, send, recv):
        x, zh, zl, y, c = coords()
        self.share, self.half_land, self.land = share, half_land, land
        right, left = device((x + 1) % 4, zh, zl, y, c), device((x + 3) % 4, zh, zl, y, c)
        far, self.near, self.back = 2 * ((x + 2) % 4), 2 * ((x + 1) % 4), 2 * ((x + 3) % 4)
        self.here, self.zh = 2 * x, zh
        moves = [
            (share.at[far], half_land.at[0], right),
            (share.at[far + 1], half_land.at[1], left),
            (share.at[pl.ds(self.near, 2)], land.at[0], right),
            (share.at[pl.ds(self.back, 2)], land.at[1], left),
        ]
        self.hops = [remote(src, dst, send.at[k], recv.at[k], to) for k, (src, dst, to) in enumerate(moves)]

    def far_out(self):
        self.hops[0].start()
        self.hops[1].start()

    def near_out(self):
        share, kind = self.share, self.share.dtype
        self.hops[0].wait_recv()
        share[self.near] = (share[self.near].astype(F32) + self.half_land[0].astype(F32)).astype(kind)
        self.hops[2].start()
        self.hops[1].wait_recv()
        share[self.back + 1] = (share[self.back + 1].astype(F32) + self.half_land[1].astype(F32)).astype(kind)
        self.hops[3].start()

    def totals(self, both):
        self.hops[2].wait_recv()
        self.hops[3].wait_recv()
        for i, k in enumerate((1 - self.zh, self.zh)):
            total = self.share[self.here + k].astype(F32)
            total += self.land[0, k].astype(F32) + self.land[1, k].astype(F32)
            both[i] = total.astype(both.dtype)

    def finish(self):
        for hop in self.hops:
            hop.wait_send()

    @staticmethod
    def scratch(r, w, kind):
        return [
            pltpu.VMEM((2, r, w), kind),
            pltpu.VMEM((2, 2, r, w), kind),
            pltpu.SemaphoreType.DMA((4,)),
            pltpu.SemaphoreType.DMA((4,)),
        ]


class PartnerSum:
    def __init__(self, both, out, land, stage, send, recv, tsend, trecv, local):
        x, zh, zl, y, c = coords()
        self.both, self.land, self.stage = both, land, stage
        self.high = remote(both.at[0], land.at[0], send.at[0], recv.at[0], device(x, 1 - zh, zl, y, c))
        self.low = remote(stage.at[0], land.at[1], send.at[1], recv.at[1], device(x, zh, 1 - zl, y, c))
        self.gather = TeamGather(stage.at[1], block_part(out), tsend, trecv, local)

    def z_out(self):
        self.high.start()

    def z_lo_out(self):
        self.high.wait()
        self.stage[0] = (self.both[1].astype(F32) + self.land[0].astype(F32)).astype(self.stage.dtype)
        self.low.start()

    def team_out(self):
        self.low.wait()
        self.stage[1] = (self.stage[0].astype(F32) + self.land[1].astype(F32)).astype(self.stage.dtype)
        self.gather.start()

    @staticmethod
    def scratch(r, w, kind):
        return [
            pltpu.VMEM((2, r, w), kind),
            pltpu.VMEM((2, r, w), kind),
            pltpu.SemaphoreType.DMA((2,)),
            pltpu.SemaphoreType.DMA((2,)),
            pltpu.SemaphoreType.DMA((9,)),
            pltpu.SemaphoreType.DMA((9,)),
            pltpu.SemaphoreType.DMA(()),
        ]


def pick(i, values):
    out = values[-1]
    for k in range(len(values) - 2, -1, -1):
        out = jnp.where(i == k, values[k], out)
    return out


def front_kernel(
    tokens, cotangent, gain_one, in_weight, taps_own, out_own, gain_two, gate_weight, up_weight, down_weight,
    tok_hbm, e, w_in_hbm, w_out, w_gu, w_down, gains, p_hbm, v_hbm, z,
    small, small_own, in_own, gu_own, down_own, z_own, tok, w_in, p, v,
    tsend, trecv, gsend, grecv, local, hsend, hrecv, saving,
):
    x, zh, zl, y, c = coords()
    member = 2 * y + c
    meet(team_peers() + x_peers() + [device(x, 1 - zh, zl, y, c)])
    tok_job = TeamGather(tokens, block_part(tok), tsend.at[0], trecv.at[0], local.at[0])
    e_job = TeamGather(cotangent, block_part(e), tsend.at[1], trecv.at[1], local.at[1])
    z_job = TeamGather(z_own, lane_part(z), tsend.at[2], trecv.at[2], local.at[2])
    out_rows = pl.ds(pl.multiple_of(c * 64, 64), 64)
    slots = [
        lambda k: small.at[k],
        lambda k: w_in.at[pl.ds(pl.multiple_of(k * 128, 128), 128)],
        lambda k: w_out.at[k, out_rows],
        lambda k: w_gu.at[k],
        lambda k: w_down.at[k],
    ]
    owned = [small_own, in_own, out_own.at[out_rows], gu_own, down_own]
    jobs = [
        GroupGather(src, slot, gsend.at[i], grecv.at[i], local.at[3 + i])
        for i, (src, slot) in enumerate(zip(owned, slots))
    ]
    tok_job.start()
    rows = [gain_one[...].astype(F32), gain_two[...].astype(F32), taps_own[...].astype(F32)]
    small_own[...] = jnp.concatenate(rows + [jnp.zeros((11, 128), F32)], axis=0).astype(BF)
    for part in range(3):
        in_own[:, 128 * part : 128 * part + 128] = in_weight[
            :, pl.ds(pl.multiple_of(part * D + member * 128, 128), 128)
        ]
    for job in jobs[:3]:
        job.start()
    place = lax.broadcasted_iota(jnp.int32, (576, PAD), 1)
    source = lax.broadcasted_iota(jnp.int32, (576, PAD), 0)
    chosen = ((place < SEG) & (source == member * SEG + place)).astype(F32).astype(BF)
    for half, weight in ((0, gate_weight), (FS, up_weight)):
        for g in range(8):
            gu_own[:, half + PAD * g : half + PAD * g + PAD] = dot(
                weight[:, 576 * g : 576 * g + 576], chosen
            ).astype(BF)
    down_own[...] = contract_rows(chosen, down_weight[...]).astype(BF)
    for job in jobs[:3]:
        job.step()
    for job in jobs[:3]:
        job.relay()
    for job in jobs[3:]:
        job.start()
    tok_job.step()
    e_job.start()
    jobs[0].finish()
    jobs[1].finish()
    for g in range(8):
        gains[:, 128 * g : 128 * g + 128] = small[g].astype(F32)
    taps = gains[:, pl.ds(pl.multiple_of(member * 128, 128), 128)]

    def project(i, carry):
        b = 2 * ((y + pick(i // 2, (0, 1, 3, 2))) % 4) + i % 2
        h0 = tok[b].astype(F32)
        n1 = (h0 * rms_scale(h0) * gains[0:1]).astype(BF)
        p[pl.ds(pl.multiple_of(b * ROWS, ROWS), ROWS)] = dot(n1, w_in[...])
        return carry

    tok_job.near_done()
    lax.fori_loop(0, 6, project, 0)
    tok_job.hand()
    tok_job.far_done()
    lax.fori_loop(6, 8, project, 0)
    for job in jobs[3:]:
        job.step()

    def convolve(b, last):
        rows = pl.ds(pl.multiple_of(b * ROWS, ROWS), ROWS)
        block = p[rows]
        mixed = block[:, :128] * block[:, 256:]
        behind = jnp.concatenate([last, mixed], axis=0)
        conv = taps[2:3] * behind[6 : ROWS + 6] + taps[3:4] * behind[7 : ROWS + 7] + taps[4:5] * behind[8:]
        v[rows] = conv
        z_own[rows] = (block[:, 128:256] * conv).astype(BF)
        return mixed[ROWS - 8 :]

    lax.fori_loop(0, 8, convolve, jnp.zeros((8, 128), F32))
    z_job.start()
    saved = [
        pltpu.make_async_copy(src, dst, saving.at[i])
        for i, (src, dst) in enumerate(((tok, tok_hbm), (w_in, w_in_hbm), (p, p_hbm), (v, v_hbm)))
    ]
    for copy in saved:
        copy.start()
    e_job.step()
    jobs[3].relay()
    jobs[4].relay()
    jobs[2].finish()
    handed = remote(w_out.at[:, out_rows], w_out.at[:, out_rows], hsend, hrecv, device(x, zh, zl, y, 1 - c))
    handed.start()
    e_job.finish()
    z_job.step()
    z_job.finish()
    other_rows = pl.ds(pl.multiple_of(64 - c * 64, 64), 64)
    jobs[3].finish()
    jobs[4].finish()
    for copy in saved:
        copy.wait()
    handed.wait_send()
    remote(w_out.at[:, out_rows], w_out.at[:, other_rows], hsend, hrecv, device(x, zh, zl, y, 1 - c)).wait_recv()


def front(args, collective_id, name):
    vmem, anywhere = pl.BlockSpec(memory_space=pltpu.VMEM), pl.BlockSpec(memory_space=pl.ANY)
    shape = jax.ShapeDtypeStruct
    return pl.pallas_call(
        front_kernel,
        out_shape=[
            shape((TEAM, ROWS, D), BF),
            shape((TEAM, ROWS, D), BF),
            shape((D, 384), BF),
            shape((8, 128, D), BF),
            shape((8, 128, 2 * FS), BF),
            shape((8, PAD, D), BF),
            shape((16, D), F32),
            shape((T, 384), F32),
            shape((T, 128), F32),
            shape((T, D), BF),
        ],
        in_specs=[vmem] * 10,
        out_specs=[anywhere] * 6 + [vmem] + [anywhere] * 3,
        scratch_shapes=[
            pltpu.VMEM((8, 16, 128), BF),
            pltpu.VMEM((16, 128), BF),
            pltpu.VMEM((128, 384), BF),
            pltpu.VMEM((128, 2 * FS), BF),
            pltpu.VMEM((PAD, D), BF),
            pltpu.VMEM((T, 128), BF),
            pltpu.VMEM((TEAM, ROWS, D), BF),
            pltpu.VMEM((D, 384), BF),
            pltpu.VMEM((T, 384), F32),
            pltpu.VMEM((T, 128), F32),
            pltpu.SemaphoreType.DMA((3, 9)),
            pltpu.SemaphoreType.DMA((3, 9)),
            pltpu.SemaphoreType.DMA((5, 7)),
            pltpu.SemaphoreType.DMA((5, 7)),
            pltpu.SemaphoreType.DMA((8,)),
            pltpu.SemaphoreType.DMA(()),
            pltpu.SemaphoreType.DMA(()),
            pltpu.SemaphoreType.DMA((4,)),
        ],
        compiler_params=pltpu.CompilerParams(
            collective_id=collective_id, has_side_effects=True, vmem_limit_bytes=VLIM
        ),
        name=name,
    )(*args)


class TeamSum:
    def __init__(self, share, pair_land, half_land, land, psend, precv, send, recv):
        x, zh, zl, y, c = coords()
        self.share, self.pair_land, self.half_land, self.land = share, pair_land, half_land, land
        sibling = device(x, zh, zl, y, 1 - c)
        right, left = device(x, zh, zl, (y + 1) % 4, c), device(x, zh, zl, (y + 3) % 4, c)
        chips = [(y + d) % 4 for d in (2, 1, 3, 0)]
        self.mine = [2 * k + c for k in chips]
        self.pairs = [
            remote(share.at[2 * chips[s] + 1 - c], pair_land.at[s], psend.at[s], precv.at[s], sibling)
            for s in range(4)
        ]
        half = ROWS // 2
        far, near, back = self.mine[0], self.mine[1], self.mine[2]
        self.hops = [
            remote(share.at[far, pl.ds(0, half)], half_land.at[0], send.at[0], recv.at[0], right),
            remote(share.at[far, pl.ds(half, half)], half_land.at[1], send.at[1], recv.at[1], left),
            remote(share.at[near], land.at[0], send.at[2], recv.at[2], right),
            remote(share.at[back], land.at[1], send.at[3], recv.at[3], left),
        ]

    def send_pair(self, s):
        self.pairs[s].start()

    def add_pair(self, s):
        share, b = self.share, self.mine[s]
        half = ROWS // 2
        self.pairs[s].wait_recv()
        total = share[b].astype(F32) + self.pair_land[s].astype(F32)
        if s in (1, 2):
            self.hops[s - 1].wait_recv()
            rows = self.half_land[s - 1].astype(F32)
            top, low = total[:half], total[half:]
            if s == 1:
                share[b, :half] = (top + rows).astype(BF)
                share[b, half:] = low.astype(BF)
            else:
                share[b, :half] = top.astype(BF)
                share[b, half:] = (low + rows).astype(BF)
            self.hops[s + 1].start()
        else:
            share[b] = total.astype(BF)
            if s == 0:
                self.hops[0].start()
                self.hops[1].start()

    def result(self):
        for pair in self.pairs:
            pair.wait_send()
        for k in (0, 1):
            self.hops[k].wait_send()
        for k in (2, 3):
            self.hops[k].wait()
        b = self.mine[3]
        return self.share[b].astype(F32) + self.land[0].astype(F32) + self.land[1].astype(F32)

    @staticmethod
    def scratch(n):
        return [
            pltpu.VMEM((n, 4, ROWS, D), BF),
            pltpu.VMEM((n, 2, ROWS // 2, D), BF),
            pltpu.VMEM((n, 2, ROWS, D), BF),
            pltpu.SemaphoreType.DMA((n, 4)),
            pltpu.SemaphoreType.DMA((n, 4)),
            pltpu.SemaphoreType.DMA((n, 4)),
            pltpu.SemaphoreType.DMA((n, 4)),
        ]


def ffn_kernel(
    tok_hbm, e_hbm, z_hbm, w_out_hbm, w_gu_hbm, w_down_hbm, gain_ref,
    block_out, dh1_out, do_hbm, gu_both, d_down_hbm, gain_grad,
    tok, e, z, w_out, w_gu, w_down, n2, a, dgq, h1_ref, do_own, share, local, wlocal, blocal,
    dsend, drecv, pair_land, half_land, land, psend, precv, send, recv, *rings,
):
    x, zh, zl, y, c = coords()
    weights = [
        pltpu.make_async_copy(src, dst, wlocal.at[i])
        for i, (src, dst) in enumerate(((w_out_hbm, w_out), (w_gu_hbm, w_gu), (w_down_hbm, w_down)))
    ]
    right, left, across = 2 * ((y + 1) % 4), 2 * ((y + 3) % 4), 2 * ((y + 2) % 4)
    order = ((across, across + 1), (right, left), (right + 1, left + 1), (2 * y, 2 * y + 1))
    blocks = []
    for s, pair in enumerate(order):
        copies = []
        for i, b in enumerate(pair):
            rows = pl.ds(pl.multiple_of(ROWS * b, ROWS), ROWS)
            copies.append(
                [
                    pltpu.make_async_copy(z_hbm.at[rows], z.at[s % 2, pl.ds(i * ROWS, ROWS)], blocal.at[s, i, 0]),
                    pltpu.make_async_copy(tok_hbm.at[b], tok.at[s % 2, i], blocal.at[s, i, 1]),
                    pltpu.make_async_copy(e_hbm.at[b], e.at[b], blocal.at[s, i, 2]),
                ]
            )
        blocks.append([copies[0][0], copies[1][0], copies[0][1], copies[1][1], copies[0][2], copies[1][2]])
    weights[0].start()
    for copy in blocks[0]:
        copy.start()
    for copy in weights[1:]:
        copy.start()
    for s, copies in enumerate(blocks[1:]):
        for i, copy in enumerate(copies):
            if i >= 4 or s == 0:
                copy.start()
    meet(team_peers() + x_peers())
    gu = RingSum(w_gu, *rings)
    sums = [
        TeamSum(
            share.at[k], pair_land.at[k], half_land.at[k], land.at[k],
            psend.at[k], precv.at[k], send.at[k], recv.at[k],
        )
        for k in range(2)
    ]
    for copy in weights:
        copy.wait()
    gain = gain_ref[1:2]
    gain_grad[...] = jnp.zeros_like(gain_grad)

    def step(s, carry):
        for k in range(4):

            @pl.when(s == k)
            def _():
                for copy in blocks[k]:
                    copy.wait()
                if k in (1, 2):
                    for copy in blocks[k + 1][:4]:
                        copy.start()

        both = [pick(s, [pair[i] for pair in order]) for i in range(2)]
        places = [pl.ds(pl.multiple_of(b * ROWS, ROWS), ROWS) for b in both]
        h1 = tok[s % 2].reshape(2 * ROWS, D).astype(F32) + dot(z[s % 2], w_out[...])
        h1_ref[...] = h1.reshape(2, ROWS, D)
        n2_b = (h1 * rms_scale(h1) * gain).astype(BF)
        for i in range(2):
            n2[places[i], :] = n2_b[i * ROWS : (i + 1) * ROWS]
        g = dot(n2_b, w_gu[:, :, :FS].reshape(D, FS))
        q = dot(n2_b, w_gu[:, :, FS:].reshape(D, FS))
        sig = jax.nn.sigmoid(g)
        act = g * sig
        a_b = (act * q).astype(BF)
        e_b = jnp.concatenate([e[both[0]], e[both[1]]], axis=0)
        da = back_project(e_b, w_down[...].reshape(FS, D))
        dg = (da * q * sig * (1.0 + g * (1.0 - sig))).astype(BF)
        dq = (da * act).astype(BF)
        for i in range(2):
            half = slice(i * ROWS, (i + 1) * ROWS)
            a[places[i], :] = a_b[half]
            dgq[places[i], :FS] = dg[half]
            dgq[places[i], FS:] = dq[half]

        @pl.when(s == 1)
        def _():
            sums[0].add_pair(0)

        @pl.when((s == 2) & (c == 0))
        def _():
            sums[0].add_pair(1)
            sums[0].add_pair(2)

        @pl.when((s == 3) & (c == 1))
        def _():
            sums[0].add_pair(1)
            sums[0].add_pair(2)

        for i in range(2):
            dn2 = back_project(dgq[places[i], :], w_gu[...].reshape(D, 2 * FS))
            share[0, both[i]] = dn2.astype(BF)
            h1 = h1_ref[i]
            gain_grad[...] += jnp.sum(dn2 * (h1 * rms_scale(h1)), axis=0, keepdims=True)
            share[1, both[i]] = dot(a[places[i], :], w_down[...].reshape(FS, D)).astype(BF)

        for k in (0, 3):

            @pl.when(s == k)
            def _():
                for job in sums:
                    job.send_pair(k)

        for core in range(2):

            @pl.when((s == 1 + core) & (c != core))
            def _():
                for job in sums:
                    job.send_pair(1)
                    job.send_pair(2)

        @pl.when(s == 1)
        def _():
            sums[1].add_pair(0)

        @pl.when((s == 2) & (c == 0))
        def _():
            sums[1].add_pair(1)
            sums[1].add_pair(2)

        @pl.when((s == 3) & (c == 1))
        def _():
            sums[1].add_pair(1)
            sums[1].add_pair(2)

        return carry

    lax.fori_loop(0, 4, step, 0)

    def tile(i, carry):
        m = (((x + 2) % 4) // 2 + i) % 2
        columns = pl.ds(pl.multiple_of(m * 512, 512), 512)
        w_gu[pl.ds(4 * m, 4)] = contract_rows(n2[:, columns], dgq[...]).astype(BF).reshape(4, 128, 2 * FS)

        @pl.when(i == 0)
        def _():
            gu.far_out()

        return carry

    lax.fori_loop(0, 2, tile, 0)
    sums[0].add_pair(3)
    w_down[...] = contract_rows(a[...], e[...].reshape(T, D)).astype(BF).reshape(8, PAD, D)
    d_down_out = pltpu.make_async_copy(w_down, d_down_hbm, wlocal.at[2])
    d_down_out.start()
    gu.near_out()
    dn2 = sums[0].result()
    h1 = h1_ref[c]
    dh1 = e[2 * y + c].astype(F32) + norm_reverse(h1, rms_scale(h1), gain, dn2)
    dh1_out[...] = dh1
    do_own[...] = dh1.astype(BF)
    do_job = TeamGather(do_own, block_part(do_hbm), dsend, drecv, local)
    do_job.start()
    sums[1].add_pair(3)
    do_job.step()
    block_out[...] = (h1_ref[c] + sums[1].result()).astype(BF)
    do_job.finish()
    gu.totals(gu_both)
    gu.finish()
    d_down_out.wait()


def ffn(tok, e, z, w_out, w_gu, w_down, gain, collective_id, name):
    vmem, anywhere = pl.BlockSpec(memory_space=pltpu.VMEM), pl.BlockSpec(memory_space=pl.ANY)
    shape = jax.ShapeDtypeStruct
    return pl.pallas_call(
        ffn_kernel,
        out_shape=[
            shape((ROWS, D), BF),
            shape((ROWS, D), F32),
            shape((TEAM, ROWS, D), BF),
            shape((2, 128, 2 * FS), BF),
            shape((8, PAD, D), BF),
            shape((1, D), F32),
        ],
        in_specs=[anywhere] * 6 + [vmem],
        out_specs=[vmem, vmem, anywhere, vmem, anywhere, vmem],
        scratch_shapes=[
            pltpu.VMEM((2, 2, ROWS, D), BF),
            pltpu.VMEM((TEAM, ROWS, D), BF),
            pltpu.VMEM((2, 2 * ROWS, D), BF),
            pltpu.VMEM((D, D), BF),
            pltpu.VMEM((8, 128, 2 * FS), BF),
            pltpu.VMEM((8, PAD, D), BF),
            pltpu.VMEM((T, D), BF),
            pltpu.VMEM((T, FS), BF),
            pltpu.VMEM((T, 2 * FS), BF),
            pltpu.VMEM((2, ROWS, D), F32),
            pltpu.VMEM((ROWS, D), BF),
            pltpu.VMEM((2, TEAM, ROWS, D), BF),
            pltpu.SemaphoreType.DMA(()),
            pltpu.SemaphoreType.DMA((3,)),
            pltpu.SemaphoreType.DMA((4, 2, 3)),
            pltpu.SemaphoreType.DMA((9,)),
            pltpu.SemaphoreType.DMA((9,)),
        ]
        + TeamSum.scratch(2)
        + RingSum.scratch(128, 2 * FS, BF),
        compiler_params=pltpu.CompilerParams(
            collective_id=collective_id, has_side_effects=True, vmem_limit_bytes=VLIM
        ),
        name=name,
    )(tok, e, z, w_out, w_gu, w_down, gain)


def conv_back_kernel(
    tok_hbm, do_hbm, z_hbm, w_out_hbm, gu_both, d_down, w_in, p, v, dh1, gains, gain_two_grad,
    token_grad, gu_out, down_out, in_out, out_out, small_out,
    tok, do, z, d_in, d_out, d_small, down_both, in_both, out_both, small_both, w_out_t, n1, up, dv, dp, sums, share, local, *rest,
):
    x, zh, zl, y, c = coords()
    member = 2 * y + c
    meet(team_peers() + x_peers() + [device(x, 1 - zh, zl, y, c), device(x, zh, 1 - zl, y, c)])
    loads = [
        pltpu.make_async_copy(src, dst, local.at[i])
        for i, (src, dst) in enumerate(
            (
                (w_out_hbm.at[pl.ds(pl.multiple_of(member * 128, 128), 128)], w_out_t),
                (do_hbm, do),
                (tok_hbm, tok),
                (z_hbm, z),
            )
        )
    ]
    for copy in loads:
        copy.start()
    dn1_sum = TeamSum(share, *[ref.at[0] for ref in rest[:7]])
    down_ring, in_ring, out_ring, small_ring = [
        RingSum(ref, *rest[7 + 4 * i : 11 + 4 * i]) for i, ref in enumerate((d_down, d_in, d_out, d_small))
    ]
    parts = (
        (gu_both, gu_out), (down_both, down_out), (in_both, in_out), (out_both, out_out), (small_both, small_out)
    )
    jobs = [PartnerSum(*part, *rest[23 + 7 * i : 30 + 7 * i]) for i, part in enumerate(parts)]
    gu, down, in_job, out_job, small = jobs
    gu.z_out()
    down_ring.far_out()
    loads[0].wait()
    loads[1].wait()
    taps = gains[:, pl.ds(pl.multiple_of(member * 128, 128), 128)]

    up[pl.ds(0, 8)] = jnp.zeros((8, 128), F32)
    dv[pl.ds(T, 8)] = jnp.zeros((8, 128), F32)

    def first(b, carry):
        rows = pl.ds(pl.multiple_of(b * ROWS, ROWS), ROWS)
        dz = back_project(do[b], w_out_t[...])
        up[pl.ds(pl.multiple_of(b * ROWS, ROWS) + 8, ROWS)] = p[rows, :128] * p[rows, 256:]
        dp[rows, 128:256] = (dz * v[rows]).astype(BF)
        dv[rows] = dz * p[rows, 128:256]
        return carry

    lax.fori_loop(0, 8, first, 0)
    loads[2].wait()
    sums[...] = jnp.zeros_like(sums)

    def second(b, carry):
        rows = pl.ds(pl.multiple_of(b * ROWS, ROWS), ROWS)
        longer = pl.ds(pl.multiple_of(b * ROWS, ROWS), ROWS + 8)
        ahead, behind = dv[longer], up[longer]
        du = taps[2:3] * ahead[2 : ROWS + 2] + taps[3:4] * ahead[1 : ROWS + 1] + taps[4:5] * ahead[:ROWS]
        dp[rows, :128] = (du * p[rows, 256:]).astype(BF)
        dp[rows, 256:] = (du * p[rows, :128]).astype(BF)
        for k in range(3):
            sums[2 + k : 3 + k, :128] += jnp.sum(
                ahead[:ROWS] * behind[6 + k : 6 + k + ROWS], axis=0, keepdims=True
            )
        h0 = tok[b].astype(F32)
        n1[rows, :] = (h0 * rms_scale(h0) * gains[0:1]).astype(BF)
        return carry

    lax.fori_loop(0, 8, second, 0)
    down_ring.near_out()
    gu.z_lo_out()
    def third(i, carry):
        s, own = i // 2, i % 2
        turn = jnp.where(s == 0, 2, jnp.where(s == 1, 1, jnp.where(s == 2, 3, 0)))
        b = 2 * ((y + turn) % 4) + jnp.where(own == 1, c, 1 - c)
        rows = pl.ds(pl.multiple_of(b * ROWS, ROWS), ROWS)
        h0 = tok[b].astype(F32)
        hs = h0 * rms_scale(h0)
        dn1 = back_project(dp[rows, :], w_in[...])
        share[b] = dn1.astype(BF)
        sums[0:1] += jnp.sum(dn1 * hs, axis=0, keepdims=True)
        for k in range(4):

            @pl.when(i == 2 * k)
            def _():
                dn1_sum.send_pair(k)

            @pl.when(i == 2 * k + 2)
            def _():
                dn1_sum.add_pair(k)

        return carry

    lax.fori_loop(0, 8, third, 0)
    down_ring.totals(down_both)
    down.z_out()
    gu.team_out()
    dn1_sum.add_pair(3)
    d_in[...] = contract_rows(n1[...], dp[...]).astype(BF).reshape(8, 128, 384)
    in_ring.far_out()
    down.z_lo_out()
    loads[3].wait()
    d_out[...] = (
        contract_rows(z[...], do[:, :, pl.ds(pl.multiple_of(member * 128, 128), 128)].reshape(T, 128))
        .astype(BF)
        .reshape(8, 128, 128)
    )
    out_ring.far_out()
    down.team_out()
    conv = sums[2:5, :128]
    for g in range(8):
        d_small[g] = jnp.zeros((16, 128), F32)
        d_small[g, 0:1] = sums[0:1, 128 * g : 128 * g + 128]
        d_small[g, 1:2] = gain_two_grad[:, 128 * g : 128 * g + 128]
        d_small[g, 2:5] = jnp.where(member == g, conv, 0.0)
    small_ring.far_out()
    in_ring.near_out()
    gu.gather.step()
    out_ring.near_out()
    small_ring.near_out()
    down.gather.step()
    in_ring.totals(in_both)
    in_job.z_out()
    out_ring.totals(out_both)
    out_job.z_out()
    small_ring.totals(small_both)
    small.z_out()
    gu.gather.hand()
    in_job.z_lo_out()
    out_job.z_lo_out()
    down.gather.hand()
    in_job.team_out()
    small.z_lo_out()
    out_job.team_out()
    small.team_out()
    late = (in_job, out_job, small)
    for job in late:
        job.gather.step()
    h0 = tok[member].astype(F32)
    token_grad[...] = dh1[...] + norm_reverse(h0, rms_scale(h0), gains[0:1], dn1_sum.result())
    for job in late:
        job.gather.hand()
    for job in jobs:
        job.gather.near_done()
        job.gather.far_done()
    for ring in (down_ring, out_ring, in_ring, small_ring):
        ring.finish()


def x_peers():
    x, zh, zl, y, c = coords()
    return [device((x + 1) % 4, zh, zl, y, c), device((x + 3) % 4, zh, zl, y, c)]


def conv_back(args, collective_id, name):
    vmem, anywhere = pl.BlockSpec(memory_space=pltpu.VMEM), pl.BlockSpec(memory_space=pl.ANY)
    shape = jax.ShapeDtypeStruct
    blocks = [((128, 2 * FS), BF), ((PAD, D), BF), ((128, 384), BF), ((128, 128), BF), ((16, 128), F32)]
    scratch = [
        pltpu.VMEM((TEAM, ROWS, D), BF),
        pltpu.VMEM((TEAM, ROWS, D), BF),
        pltpu.VMEM((T, D), BF),
    ]
    scratch += [pltpu.VMEM((8,) + block, kind) for block, kind in blocks[2:]]
    scratch += [pltpu.VMEM((2,) + block, kind) for block, kind in blocks[1:]]
    scratch += [
        pltpu.VMEM((128, D), BF),
        pltpu.VMEM((T, D), BF),
        pltpu.VMEM((T + 8, 128), F32),
        pltpu.VMEM((T + 8, 128), F32),
        pltpu.VMEM((T, 384), BF),
        pltpu.VMEM((8, D), F32),
        pltpu.VMEM((TEAM, ROWS, D), BF),
        pltpu.SemaphoreType.DMA((4,)),
    ]
    scratch += TeamSum.scratch(1)
    for block, kind in blocks[1:]:
        scratch += RingSum.scratch(*block, kind)
    for block, kind in blocks:
        scratch += PartnerSum.scratch(*block, kind)
    return pl.pallas_call(
        conv_back_kernel,
        out_shape=[shape((ROWS, D), F32)] + [shape((8,) + block, kind) for block, kind in blocks],
        in_specs=[anywhere] * 4 + [vmem] * 8,
        out_specs=[vmem] + [anywhere] * 5,
        scratch_shapes=scratch,
        compiler_params=pltpu.CompilerParams(
            collective_id=collective_id, has_side_effects=True, vmem_limit_bytes=VLIM
        ),
        name=name,
    )(*args)


def assemble_kernel(gu, down, w_in, w_out, small, block, token, g_in, g_out, g_gate, g_up, g_down, g_one, g_two, g_conv, b_out, t_out):
    for t in range(TEAM):
        for part in range(3):
            at = part * D + 128 * t
            g_in[:, at : at + 128] = w_in[t, :, 128 * part : 128 * part + 128].astype(F32)
        g_out[:, 128 * t : 128 * t + 128] = w_out[t].astype(F32)
    for t in range(2):
        g_down[SEG * t : SEG * t + SEG, :] = down[t, :SEG].astype(F32)
    total = small[0]
    for t in range(1, TEAM):
        total += small[t]
    g_one[...] = total[0:1]
    g_two[...] = total[1:2]
    g_conv[...] = total[2:5]
    b_out[...] = block[...]
    t_out[...] = token[...]
    pieces = [gu[t].astype(F32) for t in range(TEAM)]
    for half, ref in ((0, g_gate), (FS, g_up)):
        for g in range(8):
            for t in range(TEAM):
                at = 576 * g + SEG * t
                ref[:, at : at + SEG] = pieces[t][:, half + PAD * g : half + PAD * g + SEG]


def assemble(gu, down, w_in, w_out, small, block, token):
    shape = jax.ShapeDtypeStruct

    def rows(count, width):
        return pl.BlockSpec((count, width), lambda i: (i, 0))

    def members(count, width):
        return pl.BlockSpec((TEAM, count, width), lambda i: (0, i, 0))

    def whole(*dims):
        return pl.BlockSpec(dims, lambda i: (0,) * len(dims))

    return pl.pallas_call(
        assemble_kernel,
        out_shape=[
            shape((128, 3 * D), F32),
            shape((128, D), F32),
            shape((128, 8 * 576), F32),
            shape((128, 8 * 576), F32),
            shape((576, D), F32),
            shape((1, 128), F32),
            shape((1, 128), F32),
            shape((3, 128), F32),
            shape((ROWS, D), BF),
            shape((ROWS, D), F32),
        ],
        grid=(4,),
        in_specs=[
            members(32, 2 * FS),
            pl.BlockSpec((2, PAD, D), lambda i: (i, 0, 0)),
            members(32, 384),
            members(32, 128),
            whole(TEAM, 16, 128),
            rows(64, D),
            rows(64, D),
        ],
        out_specs=[
            rows(32, 3 * D),
            rows(32, D),
            rows(32, 8 * 576),
            rows(32, 8 * 576),
            rows(144, D),
            whole(1, 128),
            whole(1, 128),
            whole(3, 128),
            rows(64, D),
            rows(64, D),
        ],
        compiler_params=pltpu.CompilerParams(vmem_limit_bytes=VLIM),
        name="assemble",
    )(gu, down, w_in, w_out, small, block, token)


def rms_scale(v):
    return lax.rsqrt(jnp.mean(v * v, axis=-1, keepdims=True) + EPSILON)


def norm_reverse(v, scale, gain, grad):
    weighted = grad * gain
    return scale * weighted - v * scale * scale * scale * jnp.mean(weighted * v, axis=-1, keepdims=True)


def dot(a, b):
    return jnp.dot(a, b, preferred_element_type=F32)


def contract_rows(left, right):
    return lax.dot_general(left, right, (((0,), (0,)), ((), ())), preferred_element_type=F32)


def back_project(grad, weight):
    return lax.dot_general(grad, weight, (((1,), (1,)), ((), ())), preferred_element_type=F32)


def on_device(
    tokens, norm_gain, in_weight, conv_weight, out_weight, ffn_gain, gate_weight, up_weight, down_weight, cotangent
):
    tok, e, w_in, w_out, w_gu, w_down, gains, p, v, z = front(
        (
            tokens, cotangent, norm_gain[None], in_weight, conv_weight, out_weight, ffn_gain[None],
            gate_weight, up_weight, down_weight,
        ),
        0,
        "front",
    )
    w_out = w_out.reshape(D, D)
    block_out, dh1, do, gu_both, d_down, d_gain_two = ffn(tok, e, z, w_out, w_gu, w_down, gains, 1, "ffn")
    token_grad, s_gu, s_down, s_in, s_out, s_small = conv_back(
        (tok, do, z, w_out, gu_both, d_down, w_in, p, v, dh1, gains, d_gain_two), 2, "conv_back"
    )
    g_in, g_out, g_gate, g_up, g_down, g_one, g_two, g_conv, block_out, token_grad = assemble(
        s_gu, s_down, s_in, s_out, s_small, block_out, token_grad
    )
    return (
        block_out, token_grad, g_one[0], g_in, g_conv, g_out, g_two[0], g_gate, g_up, g_down
    )


def solution(mesh):
    tok = P(("group", "replica"), None)
    rows = P("group", None)
    in_specs = (tok, P("group"), rows, P(None, "group"), rows, P("group"), rows, rows, rows, tok)
    out_specs = (tok, tok, P("group"), rows, P(None, "group"), rows, P("group"), rows, rows, rows)
    return jax.shard_map(on_device, mesh=mesh, in_specs=in_specs, out_specs=out_specs, check_vma=False)
```

```python
import functools

import jax
import jax.numpy as jnp
from jax import lax
from jax.experimental import pallas as pl
from jax.experimental.pallas import tpu as pltpu
from jax.sharding import PartitionSpec as P

MESH = pl.DeviceIdType.MESH
EPSILON = 1e-06
BF = jnp.bfloat16
F32 = jnp.float32
D = 1024
SEG = 72
PAD = 80
FS = 8 * PAD
TEAM = 8
ROWS = 256
T = TEAM * ROWS
VLIM = 60 * 2**20


def coords():
    group, replica = lax.axis_index("group"), lax.axis_index("replica")
    return group // 2, group % 2, replica // 8, (replica // 2) % 4, replica % 2


def device(x, zh, zl, y, c):
    return (x * 2 + zh, zl * 8 + y * 2 + c)


def remote(src, dst, send, recv, target):
    return pltpu.make_async_remote_copy(
        src_ref=src, dst_ref=dst, send_sem=send, recv_sem=recv, device_id=target, device_id_type=MESH
    )


def team_peers():
    x, zh, zl, y, c = coords()
    return [device(x, zh, zl, y, 1 - c)] + [device(x, zh, zl, (y + d) % 4, c) for d in (1, 2, 3)]


def group_peers():
    x, zh, zl, y, c = coords()
    return [
        device((x + dx) % 4, (zh + dz) % 2, zl, y, c)
        for dx in range(4)
        for dz in range(2)
        if (dx, dz) != (0, 0)
    ]


def z_peer():
    x, zh, zl, y, c = coords()
    return device(x, zh, 1 - zl, y, c)


def meet(peers):
    barrier = pltpu.get_barrier_semaphore()
    for peer in peers:
        pl.semaphore_signal(barrier, inc=1, device_id=peer, device_id_type=MESH)
    pl.semaphore_wait(barrier, len(peers))


class TeamGather:
    def __init__(self, src, part, send, recv, local):
        x, zh, zl, y, c = coords()
        sibling = device(x, zh, zl, y, 1 - c)
        right, left = device(x, zh, zl, (y + 1) % 4, c), device(x, zh, zl, (y + 3) % 4, c)
        me = 2 * y + c
        before, after, across = 2 * ((y + 3) % 4) + c, 2 * ((y + 1) % 4) + c, 2 * ((y + 2) % 4) + c
        self.own = pltpu.make_async_copy(src, part(me, None), local)

        def hop(source, block, half, k, target):
            return remote(source, part(block, half), send.at[k], recv.at[k], target)

        self.pair = hop(src, me, None, 0, sibling)
        self.out = [hop(src, me, None, 1, right), hop(src, me, None, 2, left)]
        self.near = [hop(src, before, None, 1, right), hop(src, after, None, 2, left)]
        self.onward = [
            hop(part(before, 0), before, 0, 3, right),
            hop(part(after, 1), after, 1, 4, left),
        ]
        self.far = [
            hop(part(across, 0), across, 0, 3, right),
            hop(part(across, 1), across, 1, 4, left),
        ]
        self.handed = [
            hop(part(before, None), before, None, 5, sibling),
            hop(part(after, None), after, None, 6, sibling),
            hop(part(across, 0), across, 0, 7, sibling),
            hop(part(across, 1), across, 1, 8, sibling),
        ]

    def start(self):
        for copy in self.out:
            copy.start()
        self.pair.start()
        self.own.start()

    def step(self):
        for i in range(2):
            self.near[i].wait_recv()
            self.onward[i].start()
            self.handed[i].start()

    def near_done(self):
        self.own.wait()
        self.pair.wait()
        for copy in self.handed[:2]:
            copy.wait()

    def hand(self):
        for i in range(2):
            self.far[i].wait_recv()
            self.handed[2 + i].start()

    def far_done(self):
        for copy in self.out + self.onward:
            copy.wait_send()
        for copy in self.handed[2:]:
            copy.wait()

    def finish(self):
        self.hand()
        self.near_done()
        self.far_done()


def block_part(ref):
    rows = ref.shape[1]
    unit = 8 if ref.dtype == F32 else 16
    cut = (rows // 2 + unit - 1) // unit * unit

    def part(i, half):
        if half is None:
            return ref.at[i]
        return ref.at[i, pl.ds(0, cut)] if half == 0 else ref.at[i, pl.ds(cut, rows - cut)]

    return part


def lane_part(ref):
    rows = ref.shape[0]

    def part(i, half):
        lanes = pl.ds(pl.multiple_of(i * 128, 128), 128)
        if half is None:
            return ref.at[:, lanes]
        return ref.at[pl.ds(half * (rows // 2), rows // 2), lanes]

    return part


class GroupGather:
    def __init__(self, src, slot, send, recv, local):
        x, zh, zl, y, c = coords()
        right, left = device((x + 1) % 4, zh, zl, y, c), device((x + 3) % 4, zh, zl, y, c)
        me, partner = 2 * x + zh, 2 * x + 1 - zh
        before, after, across = 2 * ((x + 3) % 4), 2 * ((x + 1) % 4), 2 * ((x + 2) % 4)
        self.own = pltpu.make_async_copy(src, slot(me), local)

        def hop(source, block, k, target):
            return remote(source, slot(block), send.at[k], recv.at[k], target)

        self.pair = hop(src, me, 0, device(x, 1 - zh, zl, y, c))
        self.out = [hop(src, me, 1, right), hop(src, me, 2, left)]
        self.paired = hop(src, partner, 0, right)
        self.second = [hop(slot(partner), partner, 3, right), hop(slot(partner), partner, 4, left)]
        self.first_in = [hop(src, before, 1 + 2 * zh, right), hop(src, after + 1, 4 - 2 * zh, left)]
        self.onward = [hop(slot(before), before, 5, right), hop(slot(after + 1), after + 1, 6, left)]
        self.last_in = [
            hop(src, before + 1, 3 - 2 * zh, right),
            hop(src, after, 2 + 2 * zh, left),
            hop(src, across, 5, right),
            hop(src, across + 1, 6, left),
        ]

    def start(self):
        self.pair.start()
        for copy in self.out:
            copy.start()
        self.own.start()

    def step(self):
        self.paired.wait_recv()
        for copy in self.second:
            copy.start()

    def relay(self):
        for i in range(2):
            self.first_in[i].wait_recv()
            self.onward[i].start()

    def finish(self):
        self.own.wait()
        for copy in self.last_in:
            copy.wait_recv()
        for copy in [self.pair] + self.out + self.second + self.onward:
            copy.wait_send()


class RingSum:
    def __init__(self, share, half_land, land, send, recv):
        x, zh, zl, y, c = coords()
        self.share, self.half_land, self.land = share, half_land, land
        right, left = device((x + 1) % 4, zh, zl, y, c), device((x + 3) % 4, zh, zl, y, c)
        far, self.near, self.back = 2 * ((x + 2) % 4), 2 * ((x + 1) % 4), 2 * ((x + 3) % 4)
        self.here, self.zh = 2 * x, zh
        moves = [
            (share.at[far], half_land.at[0], right),
            (share.at[far + 1], half_land.at[1], left),
            (share.at[pl.ds(self.near, 2)], land.at[0], right),
            (share.at[pl.ds(self.back, 2)], land.at[1], left),
        ]
        self.hops = [remote(src, dst, send.at[k], recv.at[k], to) for k, (src, dst, to) in enumerate(moves)]

    def far_out(self):
        self.hops[0].start()
        self.hops[1].start()

    def near_out(self):
        share, kind = self.share, self.share.dtype
        self.hops[0].wait_recv()
        share[self.near] = (share[self.near].astype(F32) + self.half_land[0].astype(F32)).astype(kind)
        self.hops[2].start()
        self.hops[1].wait_recv()
        share[self.back + 1] = (share[self.back + 1].astype(F32) + self.half_land[1].astype(F32)).astype(kind)
        self.hops[3].start()

    def totals(self, both):
        self.hops[2].wait_recv()
        self.hops[3].wait_recv()
        for i, k in enumerate((1 - self.zh, self.zh)):
            total = self.share[self.here + k].astype(F32)
            total += self.land[0, k].astype(F32) + self.land[1, k].astype(F32)
            both[i] = total.astype(both.dtype)

    def finish(self):
        for hop in self.hops:
            hop.wait_send()

    @staticmethod
    def scratch(r, w, kind):
        return [
            pltpu.VMEM((2, r, w), kind),
            pltpu.VMEM((2, 2, r, w), kind),
            pltpu.SemaphoreType.DMA((4,)),
            pltpu.SemaphoreType.DMA((4,)),
        ]


class PartnerSum:
    def __init__(self, both, out, land, stage, send, recv, tsend, trecv, local):
        x, zh, zl, y, c = coords()
        self.both, self.land, self.stage = both, land, stage
        self.high = remote(both.at[0], land.at[0], send.at[0], recv.at[0], device(x, 1 - zh, zl, y, c))
        self.low = remote(stage.at[0], land.at[1], send.at[1], recv.at[1], device(x, zh, 1 - zl, y, c))
        self.gather = TeamGather(stage.at[1], block_part(out), tsend, trecv, local)

    def z_out(self):
        self.high.start()

    def z_lo_out(self):
        self.high.wait()
        self.stage[0] = (self.both[1].astype(F32) + self.land[0].astype(F32)).astype(self.stage.dtype)
        self.low.start()

    def team_out(self):
        self.low.wait()
        self.stage[1] = (self.stage[0].astype(F32) + self.land[1].astype(F32)).astype(self.stage.dtype)
        self.gather.start()

    @staticmethod
    def scratch(r, w, kind):
        return [
            pltpu.VMEM((2, r, w), kind),
            pltpu.VMEM((2, r, w), kind),
            pltpu.SemaphoreType.DMA((2,)),
            pltpu.SemaphoreType.DMA((2,)),
            pltpu.SemaphoreType.DMA((9,)),
            pltpu.SemaphoreType.DMA((9,)),
            pltpu.SemaphoreType.DMA(()),
        ]


def pick(i, values):
    out = values[-1]
    for k in range(len(values) - 2, -1, -1):
        out = jnp.where(i == k, values[k], out)
    return out


def front_kernel(
    tokens, cotangent, gain_one, in_weight, taps_own, out_own, gain_two, gate_weight, up_weight, down_weight,
    tok_hbm, e, w_in_hbm, w_out, w_gu, w_down, gains, p_hbm, v_hbm, z,
    small, small_own, in_own, gu_own, down_own, z_own, tok, w_in, p, v,
    tsend, trecv, gsend, grecv, local, hsend, hrecv, saving,
):
    x, zh, zl, y, c = coords()
    member = 2 * y + c
    meet(team_peers() + x_peers() + [device(x, 1 - zh, zl, y, c)])
    tok_job = TeamGather(tokens, block_part(tok), tsend.at[0], trecv.at[0], local.at[0])
    e_job = TeamGather(cotangent, block_part(e), tsend.at[1], trecv.at[1], local.at[1])
    z_job = TeamGather(z_own, lane_part(z), tsend.at[2], trecv.at[2], local.at[2])
    out_rows = pl.ds(pl.multiple_of(c * 64, 64), 64)
    slots = [
        lambda k: small.at[k],
        lambda k: w_in.at[pl.ds(pl.multiple_of(k * 128, 128), 128)],
        lambda k: w_out.at[k, out_rows],
        lambda k: w_gu.at[k],
        lambda k: w_down.at[k],
    ]
    owned = [small_own, in_own, out_own.at[out_rows], gu_own, down_own]
    jobs = [
        GroupGather(src, slot, gsend.at[i], grecv.at[i], local.at[3 + i])
        for i, (src, slot) in enumerate(zip(owned, slots))
    ]
    tok_job.start()
    rows = [gain_one[...].astype(F32), gain_two[...].astype(F32), taps_own[...].astype(F32)]
    small_own[...] = jnp.concatenate(rows + [jnp.zeros((11, 128), F32)], axis=0).astype(BF)
    for part in range(3):
        in_own[:, 128 * part : 128 * part + 128] = in_weight[
            :, pl.ds(pl.multiple_of(part * D + member * 128, 128), 128)
        ]
    for job in jobs[:3]:
        job.start()
    place = lax.broadcasted_iota(jnp.int32, (576, PAD), 1)
    source = lax.broadcasted_iota(jnp.int32, (576, PAD), 0)
    chosen = ((place < SEG) & (source == member * SEG + place)).astype(F32).astype(BF)
    for half, weight in ((0, gate_weight), (FS, up_weight)):
        for g in range(8):
            gu_own[:, half + PAD * g : half + PAD * g + PAD] = dot(
                weight[:, 576 * g : 576 * g + 576], chosen
            ).astype(BF)
    down_own[...] = contract_rows(chosen, down_weight[...]).astype(BF)
    for job in jobs[:3]:
        job.step()
    for job in jobs[:3]:
        job.relay()
    for job in jobs[3:]:
        job.start()
    tok_job.step()
    e_job.start()
    jobs[0].finish()
    jobs[1].finish()
    for g in range(8):
        gains[:, 128 * g : 128 * g + 128] = small[g].astype(F32)
    taps = gains[:, pl.ds(pl.multiple_of(member * 128, 128), 128)]

    def project(i, carry):
        b = 2 * ((y + pick(i // 2, (0, 1, 3, 2))) % 4) + i % 2
        h0 = tok[b].astype(F32)
        n1 = (h0 * rms_scale(h0) * gains[0:1]).astype(BF)
        p[pl.ds(pl.multiple_of(b * ROWS, ROWS), ROWS)] = dot(n1, w_in[...])
        return carry

    tok_job.near_done()
    lax.fori_loop(0, 6, project, 0)
    tok_job.hand()
    tok_job.far_done()
    lax.fori_loop(6, 8, project, 0)
    for job in jobs[3:]:
        job.step()

    def convolve(b, last):
        rows = pl.ds(pl.multiple_of(b * ROWS, ROWS), ROWS)
        block = p[rows]
        mixed = block[:, :128] * block[:, 256:]
        behind = jnp.concatenate([last, mixed], axis=0)
        conv = taps[2:3] * behind[6 : ROWS + 6] + taps[3:4] * behind[7 : ROWS + 7] + taps[4:5] * behind[8:]
        v[rows] = conv
        z_own[rows] = (block[:, 128:256] * conv).astype(BF)
        return mixed[ROWS - 8 :]

    lax.fori_loop(0, 8, convolve, jnp.zeros((8, 128), F32))
    z_job.start()
    saved = [
        pltpu.make_async_copy(src, dst, saving.at[i])
        for i, (src, dst) in enumerate(((tok, tok_hbm), (w_in, w_in_hbm), (p, p_hbm), (v, v_hbm)))
    ]
    for copy in saved:
        copy.start()
    e_job.step()
    jobs[3].relay()
    jobs[4].relay()
    jobs[2].finish()
    handed = remote(w_out.at[:, out_rows], w_out.at[:, out_rows], hsend, hrecv, device(x, zh, zl, y, 1 - c))
    handed.start()
    e_job.finish()
    z_job.step()
    z_job.finish()
    other_rows = pl.ds(pl.multiple_of(64 - c * 64, 64), 64)
    jobs[3].finish()
    jobs[4].finish()
    for copy in saved:
        copy.wait()
    handed.wait_send()
    remote(w_out.at[:, out_rows], w_out.at[:, other_rows], hsend, hrecv, device(x, zh, zl, y, 1 - c)).wait_recv()


def front(args, collective_id, name):
    vmem, anywhere = pl.BlockSpec(memory_space=pltpu.VMEM), pl.BlockSpec(memory_space=pl.ANY)
    shape = jax.ShapeDtypeStruct
    return pl.pallas_call(
        front_kernel,
        out_shape=[
            shape((TEAM, ROWS, D), BF),
            shape((TEAM, ROWS, D), BF),
            shape((D, 384), BF),
            shape((8, 128, D), BF),
            shape((8, 128, 2 * FS), BF),
            shape((8, PAD, D), BF),
            shape((16, D), F32),
            shape((T, 384), F32),
            shape((T, 128), F32),
            shape((T, D), BF),
        ],
        in_specs=[vmem] * 10,
        out_specs=[anywhere] * 6 + [vmem] + [anywhere] * 3,
        scratch_shapes=[
            pltpu.VMEM((8, 16, 128), BF),
            pltpu.VMEM((16, 128), BF),
            pltpu.VMEM((128, 384), BF),
            pltpu.VMEM((128, 2 * FS), BF),
            pltpu.VMEM((PAD, D), BF),
            pltpu.VMEM((T, 128), BF),
            pltpu.VMEM((TEAM, ROWS, D), BF),
            pltpu.VMEM((D, 384), BF),
            pltpu.VMEM((T, 384), F32),
            pltpu.VMEM((T, 128), F32),
            pltpu.SemaphoreType.DMA((3, 9)),
            pltpu.SemaphoreType.DMA((3, 9)),
            pltpu.SemaphoreType.DMA((5, 7)),
            pltpu.SemaphoreType.DMA((5, 7)),
            pltpu.SemaphoreType.DMA((8,)),
            pltpu.SemaphoreType.DMA(()),
            pltpu.SemaphoreType.DMA(()),
            pltpu.SemaphoreType.DMA((4,)),
        ],
        compiler_params=pltpu.CompilerParams(
            collective_id=collective_id, has_side_effects=True, vmem_limit_bytes=VLIM
        ),
        name=name,
    )(*args)


class TeamSum:
    def __init__(self, share, pair_land, half_land, land, psend, precv, send, recv):
        x, zh, zl, y, c = coords()
        self.share, self.pair_land, self.half_land, self.land = share, pair_land, half_land, land
        sibling = device(x, zh, zl, y, 1 - c)
        right, left = device(x, zh, zl, (y + 1) % 4, c), device(x, zh, zl, (y + 3) % 4, c)
        chips = [(y + d) % 4 for d in (2, 1, 3, 0)]
        self.mine = [2 * k + c for k in chips]
        self.pairs = [
            remote(share.at[2 * chips[s] + 1 - c], pair_land.at[s], psend.at[s], precv.at[s], sibling)
            for s in range(4)
        ]
        half = ROWS // 2
        far, near, back = self.mine[0], self.mine[1], self.mine[2]
        self.hops = [
            remote(share.at[far, pl.ds(0, half)], half_land.at[0], send.at[0], recv.at[0], right),
            remote(share.at[far, pl.ds(half, half)], half_land.at[1], send.at[1], recv.at[1], left),
            remote(share.at[near], land.at[0], send.at[2], recv.at[2], right),
            remote(share.at[back], land.at[1], send.at[3], recv.at[3], left),
        ]

    def send_pair(self, s):
        self.pairs[s].start()

    def add_pair(self, s):
        share, b = self.share, self.mine[s]
        half = ROWS // 2
        self.pairs[s].wait_recv()
        total = share[b].astype(F32) + self.pair_land[s].astype(F32)
        if s in (1, 2):
            self.hops[s - 1].wait_recv()
            rows = self.half_land[s - 1].astype(F32)
            top, low = total[:half], total[half:]
            if s == 1:
                share[b, :half] = (top + rows).astype(BF)
                share[b, half:] = low.astype(BF)
            else:
                share[b, :half] = top.astype(BF)
                share[b, half:] = (low + rows).astype(BF)
            self.hops[s + 1].start()
        else:
            share[b] = total.astype(BF)
            if s == 0:
                self.hops[0].start()
                self.hops[1].start()

    def result(self):
        for pair in self.pairs:
            pair.wait_send()
        for k in (0, 1):
            self.hops[k].wait_send()
        for k in (2, 3):
            self.hops[k].wait()
        b = self.mine[3]
        return self.share[b].astype(F32) + self.land[0].astype(F32) + self.land[1].astype(F32)

    @staticmethod
    def scratch(n):
        return [
            pltpu.VMEM((n, 4, ROWS, D), BF),
            pltpu.VMEM((n, 2, ROWS // 2, D), BF),
            pltpu.VMEM((n, 2, ROWS, D), BF),
            pltpu.SemaphoreType.DMA((n, 4)),
            pltpu.SemaphoreType.DMA((n, 4)),
            pltpu.SemaphoreType.DMA((n, 4)),
            pltpu.SemaphoreType.DMA((n, 4)),
        ]


def ffn_kernel(
    tok_hbm, e_hbm, z_hbm, w_out_hbm, w_gu_hbm, w_down_hbm, gain_ref,
    block_out, dh1_out, do_hbm, gu_both, d_down_hbm, gain_grad,
    tok, e, z, w_out, w_gu, w_down, n2, a, dgq, h1_ref, do_own, share, local, wlocal, blocal,
    dsend, drecv, pair_land, half_land, land, psend, precv, send, recv, *rings,
):
    x, zh, zl, y, c = coords()
    weights = [
        pltpu.make_async_copy(src, dst, wlocal.at[i])
        for i, (src, dst) in enumerate(((w_out_hbm, w_out), (w_gu_hbm, w_gu), (w_down_hbm, w_down)))
    ]
    right, left, across = 2 * ((y + 1) % 4), 2 * ((y + 3) % 4), 2 * ((y + 2) % 4)
    order = ((across, across + 1), (right, left), (right + 1, left + 1), (2 * y, 2 * y + 1))
    blocks = []
    for s, pair in enumerate(order):
        copies = []
        for i, b in enumerate(pair):
            rows = pl.ds(pl.multiple_of(ROWS * b, ROWS), ROWS)
            copies.append(
                [
                    pltpu.make_async_copy(z_hbm.at[rows], z.at[s % 2, pl.ds(i * ROWS, ROWS)], blocal.at[s, i, 0]),
                    pltpu.make_async_copy(tok_hbm.at[b], tok.at[s % 2, i], blocal.at[s, i, 1]),
                    pltpu.make_async_copy(e_hbm.at[b], e.at[b], blocal.at[s, i, 2]),
                ]
            )
        blocks.append([copies[0][0], copies[1][0], copies[0][1], copies[1][1], copies[0][2], copies[1][2]])
    weights[0].start()
    for copy in blocks[0]:
        copy.start()
    for copy in weights[1:]:
        copy.start()
    for s, copies in enumerate(blocks[1:]):
        for i, copy in enumerate(copies):
            if i >= 4 or s == 0:
                copy.start()
    meet(team_peers() + x_peers())
    gu = RingSum(w_gu, *rings)
    sums = [
        TeamSum(
            share.at[k], pair_land.at[k], half_land.at[k], land.at[k],
            psend.at[k], precv.at[k], send.at[k], recv.at[k],
        )
        for k in range(2)
    ]
    for copy in weights:
        copy.wait()
    gain = gain_ref[1:2]
    gain_grad[...] = jnp.zeros_like(gain_grad)

    def step(s, carry):
        for k in range(4):

            @pl.when(s == k)
            def _():
                for copy in blocks[k]:
                    copy.wait()
                if k in (1, 2):
                    for copy in blocks[k + 1][:4]:
                        copy.start()

        both = [pick(s, [pair[i] for pair in order]) for i in range(2)]
        places = [pl.ds(pl.multiple_of(b * ROWS, ROWS), ROWS) for b in both]
        h1 = tok[s % 2].reshape(2 * ROWS, D).astype(F32) + dot(z[s % 2], w_out[...])
        h1_ref[...] = h1.reshape(2, ROWS, D)
        n2_b = (h1 * rms_scale(h1) * gain).astype(BF)
        for i in range(2):
            n2[places[i], :] = n2_b[i * ROWS : (i + 1) * ROWS]
        g = dot(n2_b, w_gu[:, :, :FS].reshape(D, FS))
        q = dot(n2_b, w_gu[:, :, FS:].reshape(D, FS))
        sig = jax.nn.sigmoid(g)
        act = g * sig
        a_b = (act * q).astype(BF)
        e_b = jnp.concatenate([e[both[0]], e[both[1]]], axis=0)
        da = back_project(e_b, w_down[...].reshape(FS, D))
        dg = (da * q * sig * (1.0 + g * (1.0 - sig))).astype(BF)
        dq = (da * act).astype(BF)
        for i in range(2):
            half = slice(i * ROWS, (i + 1) * ROWS)
            a[places[i], :] = a_b[half]
            dgq[places[i], :FS] = dg[half]
            dgq[places[i], FS:] = dq[half]

        @pl.when(s == 1)
        def _():
            sums[0].add_pair(0)

        @pl.when((s == 2) & (c == 0))
        def _():
            sums[0].add_pair(1)
            sums[0].add_pair(2)

        @pl.when((s == 3) & (c == 1))
        def _():
            sums[0].add_pair(1)
            sums[0].add_pair(2)

        for i in range(2):
            dn2 = back_project(dgq[places[i], :], w_gu[...].reshape(D, 2 * FS))
            share[0, both[i]] = dn2.astype(BF)
            h1 = h1_ref[i]
            gain_grad[...] += jnp.sum(dn2 * (h1 * rms_scale(h1)), axis=0, keepdims=True)
            share[1, both[i]] = dot(a[places[i], :], w_down[...].reshape(FS, D)).astype(BF)

        for k in (0, 3):

            @pl.when(s == k)
            def _():
                for job in sums:
                    job.send_pair(k)

        for core in range(2):

            @pl.when((s == 1 + core) & (c != core))
            def _():
                for job in sums:
                    job.send_pair(1)
                    job.send_pair(2)

        @pl.when(s == 1)
        def _():
            sums[1].add_pair(0)

        @pl.when((s == 2) & (c == 0))
        def _():
            sums[1].add_pair(1)
            sums[1].add_pair(2)

        @pl.when((s == 3) & (c == 1))
        def _():
            sums[1].add_pair(1)
            sums[1].add_pair(2)

        return carry

    lax.fori_loop(0, 4, step, 0)

    def tile(i, carry):
        m = (((x + 2) % 4) // 2 + i) % 2
        columns = pl.ds(pl.multiple_of(m * 512, 512), 512)
        w_gu[pl.ds(4 * m, 4)] = contract_rows(n2[:, columns], dgq[...]).astype(BF).reshape(4, 128, 2 * FS)

        @pl.when(i == 0)
        def _():
            gu.far_out()

        return carry

    lax.fori_loop(0, 2, tile, 0)
    sums[0].add_pair(3)
    w_down[...] = contract_rows(a[...], e[...].reshape(T, D)).astype(BF).reshape(8, PAD, D)
    d_down_out = pltpu.make_async_copy(w_down, d_down_hbm, wlocal.at[2])
    d_down_out.start()
    gu.near_out()
    dn2 = sums[0].result()
    h1 = h1_ref[c]
    dh1 = e[2 * y + c].astype(F32) + norm_reverse(h1, rms_scale(h1), gain, dn2)
    dh1_out[...] = dh1
    do_own[...] = dh1.astype(BF)
    do_job = TeamGather(do_own, block_part(do_hbm), dsend, drecv, local)
    do_job.start()
    sums[1].add_pair(3)
    do_job.step()
    block_out[...] = (h1_ref[c] + sums[1].result()).astype(BF)
    do_job.finish()
    gu.totals(gu_both)
    gu.finish()
    d_down_out.wait()


def ffn(tok, e, z, w_out, w_gu, w_down, gain, collective_id, name):
    vmem, anywhere = pl.BlockSpec(memory_space=pltpu.VMEM), pl.BlockSpec(memory_space=pl.ANY)
    shape = jax.ShapeDtypeStruct
    return pl.pallas_call(
        ffn_kernel,
        out_shape=[
            shape((ROWS, D), BF),
            shape((ROWS, D), F32),
            shape((TEAM, ROWS, D), BF),
            shape((2, 128, 2 * FS), BF),
            shape((8, PAD, D), BF),
            shape((1, D), F32),
        ],
        in_specs=[anywhere] * 6 + [vmem],
        out_specs=[vmem, vmem, anywhere, vmem, anywhere, vmem],
        scratch_shapes=[
            pltpu.VMEM((2, 2, ROWS, D), BF),
            pltpu.VMEM((TEAM, ROWS, D), BF),
            pltpu.VMEM((2, 2 * ROWS, D), BF),
            pltpu.VMEM((D, D), BF),
            pltpu.VMEM((8, 128, 2 * FS), BF),
            pltpu.VMEM((8, PAD, D), BF),
            pltpu.VMEM((T, D), BF),
            pltpu.VMEM((T, FS), BF),
            pltpu.VMEM((T, 2 * FS), BF),
            pltpu.VMEM((2, ROWS, D), F32),
            pltpu.VMEM((ROWS, D), BF),
            pltpu.VMEM((2, TEAM, ROWS, D), BF),
            pltpu.SemaphoreType.DMA(()),
            pltpu.SemaphoreType.DMA((3,)),
            pltpu.SemaphoreType.DMA((4, 2, 3)),
            pltpu.SemaphoreType.DMA((9,)),
            pltpu.SemaphoreType.DMA((9,)),
        ]
        + TeamSum.scratch(2)
        + RingSum.scratch(128, 2 * FS, BF),
        compiler_params=pltpu.CompilerParams(
            collective_id=collective_id, has_side_effects=True, vmem_limit_bytes=VLIM
        ),
        name=name,
    )(tok, e, z, w_out, w_gu, w_down, gain)


def conv_back_kernel(
    tok_hbm, do_hbm, z_hbm, w_out_hbm, gu_both, d_down, w_in, p, v, dh1, gains, gain_two_grad,
    token_grad, gu_out, down_out, in_out, out_out, small_out,
    tok, do, z, d_in, d_out, d_small, down_both, in_both, out_both, small_both, w_out_t, n1, up, dv, dp, sums, share, local, *rest,
):
    x, zh, zl, y, c = coords()
    member = 2 * y + c
    meet(team_peers() + x_peers() + [device(x, 1 - zh, zl, y, c), device(x, zh, 1 - zl, y, c)])
    loads = [
        pltpu.make_async_copy(src, dst, local.at[i])
        for i, (src, dst) in enumerate(
            (
                (w_out_hbm.at[pl.ds(pl.multiple_of(member * 128, 128), 128)], w_out_t),
                (do_hbm, do),
                (tok_hbm, tok),
                (z_hbm, z),
            )
        )
    ]
    for copy in loads:
        copy.start()
    dn1_sum = TeamSum(share, *[ref.at[0] for ref in rest[:7]])
    down_ring, in_ring, out_ring, small_ring = [
        RingSum(ref, *rest[7 + 4 * i : 11 + 4 * i]) for i, ref in enumerate((d_down, d_in, d_out, d_small))
    ]
    parts = (
        (gu_both, gu_out), (down_both, down_out), (in_both, in_out), (out_both, out_out), (small_both, small_out)
    )
    jobs = [PartnerSum(*part, *rest[23 + 7 * i : 30 + 7 * i]) for i, part in enumerate(parts)]
    gu, down, in_job, out_job, small = jobs
    gu.z_out()
    down_ring.far_out()
    loads[0].wait()
    loads[1].wait()
    taps = gains[:, pl.ds(pl.multiple_of(member * 128, 128), 128)]

    up[pl.ds(0, 8)] = jnp.zeros((8, 128), F32)
    dv[pl.ds(T, 8)] = jnp.zeros((8, 128), F32)

    def first(b, carry):
        rows = pl.ds(pl.multiple_of(b * ROWS, ROWS), ROWS)
        dz = back_project(do[b], w_out_t[...])
        up[pl.ds(pl.multiple_of(b * ROWS, ROWS) + 8, ROWS)] = p[rows, :128] * p[rows, 256:]
        dp[rows, 128:256] = (dz * v[rows]).astype(BF)
        dv[rows] = dz * p[rows, 128:256]
        return carry

    lax.fori_loop(0, 8, first, 0)
    loads[2].wait()
    sums[...] = jnp.zeros_like(sums)

    def second(b, carry):
        rows = pl.ds(pl.multiple_of(b * ROWS, ROWS), ROWS)
        longer = pl.ds(pl.multiple_of(b * ROWS, ROWS), ROWS + 8)
        ahead, behind = dv[longer], up[longer]
        du = taps[2:3] * ahead[2 : ROWS + 2] + taps[3:4] * ahead[1 : ROWS + 1] + taps[4:5] * ahead[:ROWS]
        dp[rows, :128] = (du * p[rows, 256:]).astype(BF)
        dp[rows, 256:] = (du * p[rows, :128]).astype(BF)
        for k in range(3):
            sums[2 + k : 3 + k, :128] += jnp.sum(
                ahead[:ROWS] * behind[6 + k : 6 + k + ROWS], axis=0, keepdims=True
            )
        h0 = tok[b].astype(F32)
        n1[rows, :] = (h0 * rms_scale(h0) * gains[0:1]).astype(BF)
        return carry

    lax.fori_loop(0, 8, second, 0)
    down_ring.near_out()
    gu.z_lo_out()
    def third(i, carry):
        s, own = i // 2, i % 2
        turn = jnp.where(s == 0, 2, jnp.where(s == 1, 1, jnp.where(s == 2, 3, 0)))
        b = 2 * ((y + turn) % 4) + jnp.where(own == 1, c, 1 - c)
        rows = pl.ds(pl.multiple_of(b * ROWS, ROWS), ROWS)
        h0 = tok[b].astype(F32)
        hs = h0 * rms_scale(h0)
        dn1 = back_project(dp[rows, :], w_in[...])
        share[b] = dn1.astype(BF)
        sums[0:1] += jnp.sum(dn1 * hs, axis=0, keepdims=True)
        for k in range(4):

            @pl.when(i == 2 * k)
            def _():
                dn1_sum.send_pair(k)

            @pl.when(i == 2 * k + 2)
            def _():
                dn1_sum.add_pair(k)

        @pl.when(i == 5)
        def _():
            gu.team_out()

        return carry

    lax.fori_loop(0, 8, third, 0)
    down_ring.totals(down_both)
    down.z_out()
    dn1_sum.add_pair(3)
    d_in[...] = contract_rows(n1[...], dp[...]).astype(BF).reshape(8, 128, 384)
    in_ring.far_out()
    down.z_lo_out()
    loads[3].wait()
    d_out[...] = (
        contract_rows(z[...], do[:, :, pl.ds(pl.multiple_of(member * 128, 128), 128)].reshape(T, 128))
        .astype(BF)
        .reshape(8, 128, 128)
    )
    out_ring.far_out()
    down.team_out()
    conv = sums[2:5, :128]
    for g in range(8):
        d_small[g] = jnp.zeros((16, 128), F32)
        d_small[g, 0:1] = sums[0:1, 128 * g : 128 * g + 128]
        d_small[g, 1:2] = gain_two_grad[:, 128 * g : 128 * g + 128]
        d_small[g, 2:5] = jnp.where(member == g, conv, 0.0)
    small_ring.far_out()
    in_ring.near_out()
    gu.gather.step()
    out_ring.near_out()
    small_ring.near_out()
    down.gather.step()
    in_ring.totals(in_both)
    in_job.z_out()
    out_ring.totals(out_both)
    out_job.z_out()
    small_ring.totals(small_both)
    small.z_out()
    gu.gather.hand()
    in_job.z_lo_out()
    out_job.z_lo_out()
    down.gather.hand()
    in_job.team_out()
    small.z_lo_out()
    out_job.team_out()
    small.team_out()
    late = (in_job, out_job, small)
    for job in late:
        job.gather.step()
    h0 = tok[member].astype(F32)
    token_grad[...] = dh1[...] + norm_reverse(h0, rms_scale(h0), gains[0:1], dn1_sum.result())
    for job in late:
        job.gather.hand()
    for job in jobs:
        job.gather.near_done()
        job.gather.far_done()
    for ring in (down_ring, out_ring, in_ring, small_ring):
        ring.finish()


def x_peers():
    x, zh, zl, y, c = coords()
    return [device((x + 1) % 4, zh, zl, y, c), device((x + 3) % 4, zh, zl, y, c)]


def conv_back(args, collective_id, name):
    vmem, anywhere = pl.BlockSpec(memory_space=pltpu.VMEM), pl.BlockSpec(memory_space=pl.ANY)
    shape = jax.ShapeDtypeStruct
    blocks = [((128, 2 * FS), BF), ((PAD, D), BF), ((128, 384), BF), ((128, 128), BF), ((16, 128), F32)]
    scratch = [
        pltpu.VMEM((TEAM, ROWS, D), BF),
        pltpu.VMEM((TEAM, ROWS, D), BF),
        pltpu.VMEM((T, D), BF),
    ]
    scratch += [pltpu.VMEM((8,) + block, kind) for block, kind in blocks[2:]]
    scratch += [pltpu.VMEM((2,) + block, kind) for block, kind in blocks[1:]]
    scratch += [
        pltpu.VMEM((128, D), BF),
        pltpu.VMEM((T, D), BF),
        pltpu.VMEM((T + 8, 128), F32),
        pltpu.VMEM((T + 8, 128), F32),
        pltpu.VMEM((T, 384), BF),
        pltpu.VMEM((8, D), F32),
        pltpu.VMEM((TEAM, ROWS, D), BF),
        pltpu.SemaphoreType.DMA((4,)),
    ]
    scratch += TeamSum.scratch(1)
    for block, kind in blocks[1:]:
        scratch += RingSum.scratch(*block, kind)
    for block, kind in blocks:
        scratch += PartnerSum.scratch(*block, kind)
    return pl.pallas_call(
        conv_back_kernel,
        out_shape=[shape((ROWS, D), F32)] + [shape((8,) + block, kind) for block, kind in blocks],
        in_specs=[anywhere] * 4 + [vmem] * 8,
        out_specs=[vmem] + [anywhere] * 5,
        scratch_shapes=scratch,
        compiler_params=pltpu.CompilerParams(
            collective_id=collective_id, has_side_effects=True, vmem_limit_bytes=VLIM
        ),
        name=name,
    )(*args)


def assemble_kernel(gu, down, w_in, w_out, small, block, token, g_in, g_out, g_gate, g_up, g_down, g_one, g_two, g_conv, b_out, t_out):
    for t in range(TEAM):
        for part in range(3):
            at = part * D + 128 * t
            g_in[:, at : at + 128] = w_in[t, :, 128 * part : 128 * part + 128].astype(F32)
        g_out[:, 128 * t : 128 * t + 128] = w_out[t].astype(F32)
    for t in range(2):
        g_down[SEG * t : SEG * t + SEG, :] = down[t, :SEG].astype(F32)
    total = small[0]
    for t in range(1, TEAM):
        total += small[t]
    g_one[...] = total[0:1]
    g_two[...] = total[1:2]
    g_conv[...] = total[2:5]
    b_out[...] = block[...]
    t_out[...] = token[...]
    pieces = [gu[t].astype(F32) for t in range(TEAM)]
    for half, ref in ((0, g_gate), (FS, g_up)):
        for g in range(8):
            for t in range(TEAM):
                at = 576 * g + SEG * t
                ref[:, at : at + SEG] = pieces[t][:, half + PAD * g : half + PAD * g + SEG]


def assemble(gu, down, w_in, w_out, small, block, token):
    shape = jax.ShapeDtypeStruct

    def rows(count, width):
        return pl.BlockSpec((count, width), lambda i: (i, 0))

    def members(count, width):
        return pl.BlockSpec((TEAM, count, width), lambda i: (0, i, 0))

    def whole(*dims):
        return pl.BlockSpec(dims, lambda i: (0,) * len(dims))

    return pl.pallas_call(
        assemble_kernel,
        out_shape=[
            shape((128, 3 * D), F32),
            shape((128, D), F32),
            shape((128, 8 * 576), F32),
            shape((128, 8 * 576), F32),
            shape((576, D), F32),
            shape((1, 128), F32),
            shape((1, 128), F32),
            shape((3, 128), F32),
            shape((ROWS, D), BF),
            shape((ROWS, D), F32),
        ],
        grid=(4,),
        in_specs=[
            members(32, 2 * FS),
            pl.BlockSpec((2, PAD, D), lambda i: (i, 0, 0)),
            members(32, 384),
            members(32, 128),
            whole(TEAM, 16, 128),
            rows(64, D),
            rows(64, D),
        ],
        out_specs=[
            rows(32, 3 * D),
            rows(32, D),
            rows(32, 8 * 576),
            rows(32, 8 * 576),
            rows(144, D),
            whole(1, 128),
            whole(1, 128),
            whole(3, 128),
            rows(64, D),
            rows(64, D),
        ],
        compiler_params=pltpu.CompilerParams(vmem_limit_bytes=VLIM),
        name="assemble",
    )(gu, down, w_in, w_out, small, block, token)


def rms_scale(v):
    return lax.rsqrt(jnp.mean(v * v, axis=-1, keepdims=True) + EPSILON)


def norm_reverse(v, scale, gain, grad):
    weighted = grad * gain
    return scale * weighted - v * scale * scale * scale * jnp.mean(weighted * v, axis=-1, keepdims=True)


def dot(a, b):
    return jnp.dot(a, b, preferred_element_type=F32)


def contract_rows(left, right):
    return lax.dot_general(left, right, (((0,), (0,)), ((), ())), preferred_element_type=F32)


def back_project(grad, weight):
    return lax.dot_general(grad, weight, (((1,), (1,)), ((), ())), preferred_element_type=F32)


def on_device(
    tokens, norm_gain, in_weight, conv_weight, out_weight, ffn_gain, gate_weight, up_weight, down_weight, cotangent
):
    tok, e, w_in, w_out, w_gu, w_down, gains, p, v, z = front(
        (
            tokens, cotangent, norm_gain[None], in_weight, conv_weight, out_weight, ffn_gain[None],
            gate_weight, up_weight, down_weight,
        ),
        0,
        "front",
    )
    w_out = w_out.reshape(D, D)
    block_out, dh1, do, gu_both, d_down, d_gain_two = ffn(tok, e, z, w_out, w_gu, w_down, gains, 1, "ffn")
    token_grad, s_gu, s_down, s_in, s_out, s_small = conv_back(
        (tok, do, z, w_out, gu_both, d_down, w_in, p, v, dh1, gains, d_gain_two), 2, "conv_back"
    )
    g_in, g_out, g_gate, g_up, g_down, g_one, g_two, g_conv, block_out, token_grad = assemble(
        s_gu, s_down, s_in, s_out, s_small, block_out, token_grad
    )
    return (
        block_out, token_grad, g_one[0], g_in, g_conv, g_out, g_two[0], g_gate, g_up, g_down
    )


def solution(mesh):
    tok = P(("group", "replica"), None)
    rows = P("group", None)
    in_specs = (tok, P("group"), rows, P(None, "group"), rows, P("group"), rows, rows, rows, tok)
    out_specs = (tok, tok, P("group"), rows, P(None, "group"), rows, P("group"), rows, rows, rows)
    return jax.shard_map(on_device, mesh=mesh, in_specs=in_specs, out_specs=out_specs, check_vma=False)
```
